256 devices in a mesh: frames: 8 (over x_hi, y), feat: 32 (over z, x_lo, core).
Axes of the slice: x: 4 (x_hi: 2, x_lo: 2; x = x_hi * 2 + x_lo), y: 4, z: 8, core: 2. Of those that a mesh axis runs over, the one named last changes fastest.
Arguments:
- frames_in: bfloat16 [8192, 440], P(('frames', 'feat')), may hold values from -8 to 8
- labels: int32 [8192], P('frames'), may hold values from 0 to 146
- projection: bfloat16 [440, 131072], P(None, 'feat'), may hold values from -0.25 to 0.25
- kernel_scale: float32 [32], P('feat'), may hold values from 0.5 to 3
- shift: float32 [131072], P('feat'), may hold values from -3.140625 to 3.140625
- weights: float32 [147, 131072], P(None, 'feat'), may hold values from -100 to 100
- readout: float32 [147, 440], replicated, may hold values from -8 to 8
Outputs:
- new_weights: float32 [147, 131072], P(None, ('feat', 'frames'))
- new_readout: float32 [147, 440], replicated
The draws below stay inside these ranges and needn't reach their ends.
All inputs are finite; a program needn't handle non-finite values.
Results may differ from the reference program's by a relative error of at most 0.0075.
Values may be sent and summed in bfloat16 or wider, within the bound.
A program may use at most 64 MiB of HBM per device.

```python
import math
import jax
import jax.numpy as jnp
from jax import lax

IN_DIM = 440
CLASSES = 147
GROUP_FEAT = 4096
GROUPS = 32
FEATURES = 131072
BATCH = 8192


def readout_shared(key):
    values = jax.random.normal(key, (CLASSES, IN_DIM), jnp.float32) * (6.0 / math.sqrt(IN_DIM))
    return jnp.clip(values, -8.0, 8.0)


def draw_readout(key, part):
    shared = readout_shared(key)
    return shared


def draw_frames_in(key, part):
    key = jax.random.fold_in(key, 3)
    keys = jax.random.split(key, 2)
    rows = jax.random.normal(keys[1], (BATCH, IN_DIM), jnp.float32)
    return jnp.clip(rows, -8.0, 8.0).astype(jnp.bfloat16)


def draw_weights(key, part):
    key = jax.random.fold_in(key, 5)
    keys = jax.random.split(key, 3)
    column = jnp.arange(FEATURES)
    within = (column % GROUP_FEAT).astype(jnp.float32) / GROUP_FEAT
    group_scale = jnp.exp(jax.random.uniform(keys[0], (GROUPS,), jnp.float32, math.log(0.4), math.log(2.0)))
    column_scale = jnp.exp(jax.random.uniform(keys[1], (FEATURES,), jnp.float32, 0.0, math.log(4.0)))
    scale = jnp.repeat(group_scale, GROUP_FEAT) * jnp.exp(math.log(3.0) * within) * column_scale
    base = jax.random.normal(keys[2], (CLASSES, FEATURES), jnp.float32)
    return jnp.clip(base * scale[None, :], -100.0, 100.0)


def set_ends(values, rng, low, top_value):
    shape = values.shape
    index_at = [jax.random.randint(jax.random.fold_in(rng, axis), (), 0, shape[axis]) for axis in range(len(shape))]
    values = values.at[tuple(index_at)].set(low)
    longest = shape.index(max(shape))
    index_at[longest] = (index_at[longest] + 1) % shape[longest]
    return values.at[tuple(index_at)].set(top_value)


def steps_of(key, dims, cuts, smallest, high):
    gain = 1.0
    for position, blocks in cuts:
        heights = jax.random.uniform(jax.random.fold_in(jax.random.fold_in(key, 6), position), (blocks,), jnp.float32, smallest / len(cuts), high / len(cuts))
        gain = gain * jnp.repeat(jnp.exp(heights), dims[position] // blocks).reshape((-1,) + (1,) * (len(dims) - 1 - position))
    return gain


def bell_draw(stream_key, shape, deviation, reach, cuts=(), kind=jnp.bfloat16):
    drawn = deviation * jax.random.normal(stream_key, shape, jnp.float32)
    if cuts:
        drawn = drawn * steps_of(stream_key, shape, cuts, -0.22, 0.18)
    return jnp.clip(drawn, -reach, reach).astype(kind)


def setup_inputs(seed: int = 0) -> dict:
    key_list = jax.random.split(jax.random.key(seed), 8)
    return {
        "frames_in": draw_frames_in(jax.random.fold_in(key_list[7], 71), 0),
        "labels": set_ends(jax.random.randint(key_list[1], (BATCH,), 0, CLASSES), jax.random.fold_in(key_list[1], 1), 0, CLASSES - 1).astype(jnp.int32),
        "projection": bell_draw(key_list[2], (IN_DIM, FEATURES), IN_DIM ** -0.5, 0.25, ((1, 32),)),
        "kernel_scale": jnp.clip(jnp.exp(math.log(3.0) - 1.7917595 * jax.random.uniform(key_list[3], (GROUPS,), jnp.float32) ** steps_of(key_list[3], (GROUPS,), ((0, 32),), -0.2, 0.2)), 0.5, 3.0),
        "shift": jnp.clip(jax.random.uniform(key_list[4], (FEATURES,), jnp.float32, -3.140625, 3.140625), -3.140625, 3.140625),
        "weights": draw_weights(jax.random.fold_in(key_list[7], 71), 0),
        "readout": draw_readout(jax.random.fold_in(key_list[7], 71), 0),
    }


def expand(frames_in, proj, scale, phase_shift):
    phase = jnp.dot(frames_in, proj, preferred_element_type=jnp.float32) * scale + phase_shift
    return (math.sqrt(2.0) * jnp.cos(phase)).astype(jnp.bfloat16)

def reference(frames_in, labels, projection, kernel_scale, shift, weights, readout):
    proj_groups = projection.reshape(IN_DIM, GROUPS, GROUP_FEAT).transpose(1, 0, 2)
    shift_groups = shift.reshape(GROUPS, GROUP_FEAT)
    weight_groups = weights.reshape(CLASSES, GROUPS, GROUP_FEAT).transpose(1, 0, 2)

    def forward(item):
        proj, scale, phase_shift, group_w = item
        feats = expand(frames_in, proj, scale, phase_shift)
        return lax.dot_general(group_w.astype(jnp.bfloat16), feats, (((1,), (1,)), ((), ())), preferred_element_type=jnp.float32)
    partial_scores = lax.optimization_barrier(jnp.sum(lax.map(forward, (proj_groups, kernel_scale, shift_groups, weight_groups)), axis=0))
    linear = jnp.dot(readout, frames_in.astype(jnp.float32).T, precision=lax.Precision.HIGHEST)
    scores = partial_scores / math.sqrt(FEATURES) + linear
    probs = jax.nn.softmax(scores, axis=0)
    onehot = (jnp.arange(CLASSES)[:, None] == labels[None, :]).astype(jnp.float32)
    residual = (probs - onehot).astype(jnp.bfloat16)
    rate = 5.0 / math.sqrt(BATCH)

    def backward(item):
        proj, scale, phase_shift, group_w = item
        feats = expand(frames_in, proj, scale, phase_shift)
        gradient = jnp.dot(residual, feats, preferred_element_type=jnp.float32)
        stepped = group_w - rate * gradient
        trimmed = jnp.sign(stepped) * jnp.maximum(jnp.abs(stepped) - 1.0, 0.0)
        group_norm = jnp.sqrt(jnp.sum(trimmed * trimmed) + 1e-06)
        return trimmed * jnp.maximum(0.0, 1.0 - 1.5 * math.sqrt(GROUP_FEAT * CLASSES) / group_norm)
    updated = lax.map(backward, (proj_groups, kernel_scale, shift_groups, weight_groups))
    new_weights = updated.transpose(1, 0, 2).reshape(CLASSES, FEATURES)
    readout_grad = jnp.dot(residual, frames_in, preferred_element_type=jnp.float32)
    new_readout = readout - 3.0 / math.sqrt(BATCH) * readout_grad
    return (new_weights, new_readout)
```

```python
import functools
import math

import jax
import jax.numpy as jnp
from jax import lax
from jax.experimental import pallas as pl
from jax.experimental.pallas import tpu as pltpu
from jax.sharding import PartitionSpec as P

MESH = pl.DeviceIdType.MESH
F32, BF16 = jnp.float32, jnp.bfloat16
LANES = 256
ROWS = 160
NB = 256

OFFS = (0, 1, -1, 2, -2, 3, -3, 4)
MIRROR = tuple(OFFS.index(-d) if -d in OFFS else OFFS.index(d) for d in OFFS)
CHUNKS = ((0, 1), (1, 3), (3, 5), (5, 7), (7, 8))

COS = (1.4142124652862549, -27.91513442993164, 91.82299041748047, -120.59228515625, 83.1423110961914, -29.799043655395508)


def features_of(product, scale, shift):
    turns = product * scale + shift
    r = turns - jnp.round(turns)
    u = r * r
    acc = COS[-1] * u + COS[-2]
    for c in COS[-3::-1]:
        acc = acc * u + c
    return acc.astype(BF16)


def kernel(
    batch, feat_total, classes,
    scale_ref, x_hbm, proj_hbm, w_hbm, labels_ref, shift_ref, readout_ref,
    out_ref, grad_out_ref,
    x_own, proj, w, w_low, x_all, feats, lab, kept, pair_out, pair_in, sum_out, sum_in,
    res_all, res_t, grad_out, grad_in, ro_t, ro_out, ro_in, ro_own, norm_out, norm_in,
    local_sem, x_send, x_recv, pair_send, pair_recv, sum_send, sum_recv, res_send, res_recv,
    grad_send, grad_recv, ro_send, ro_recv, all_send, all_recv, norm_send, norm_recv,
):
    me = lax.axis_index("feat")
    group = lax.axis_index("frames")
    z, q = me // 4, me % 4
    xh, y = group // 4, group % 4
    q_sib = q + 1 - 2 * (q % 2)
    q_x = (q + 2) % 4

    def feat_dev(d, qq):
        return {"feat": ((z + d + 8) % 8) * 4 + qq}

    def frame_dev(k):
        dx, dy = k // 4, k % 4
        return ((xh + dx) % 2) * 4 + (y + dy) % 4

    sibling, neighbour = feat_dev(0, q_sib), feat_dev(0, q_x)
    sends = []

    def send(src, dst, ssem, rsem, dev):
        copy = pltpu.make_async_remote_copy(
            src_ref=src, dst_ref=dst, send_sem=ssem, recv_sem=rsem, device_id=dev, device_id_type=MESH
        )
        copy.start()
        sends.append(copy)

    def arrived(ref, rsem):
        pltpu.make_async_remote_copy(
            src_ref=ref, dst_ref=ref, send_sem=x_send.at[0], recv_sem=rsem, device_id=sibling, device_id_type=MESH
        ).wait_recv()

    copy_x = pltpu.make_async_copy(x_hbm, x_own, local_sem.at[0])
    copy_p = pltpu.make_async_copy(proj_hbm, proj, local_sem.at[1])
    copy_w = pltpu.make_async_copy(w_hbm, w, local_sem.at[2])
    copy_x.start()
    copy_p.start()
    copy_w.start()

    barrier = pltpu.get_barrier_semaphore()
    partners = [feat_dev(d, q) for d in OFFS[1:]] + [feat_dev(d, q_x) for d in OFFS] + [sibling]
    partners += [{"frames": frame_dev(k)} for k in range(1, 8)]
    for dev in partners:
        pl.semaphore_signal(barrier, inc=1, device_id=dev, device_id_type=MESH)
    copy_x.wait()
    x_all[0, 0] = x_own[...]
    pl.semaphore_wait(barrier, len(partners))

    def gather_start(buf, ss, rs):
        for s in (7, 6, 5, 4, 3, 2, 1):
            m = MIRROR[s]
            send(buf.at[0, 0], buf.at[m, 0], ss.at[s], rs.at[m, 0], feat_dev(OFFS[s], q))
        gather_local(buf, ss, rs, 0, False)

    def gather_local(buf, ss, rs, s, wait=True):
        if wait:
            arrived(buf.at[s, 0], rs.at[s, 0])
        send(buf.at[s, 0], buf.at[s, 2], ss.at[8 + s], rs.at[s, 2], neighbour)
        send(buf.at[s, 0], buf.at[s, 1], ss.at[16 + s], rs.at[s, 1], sibling)

    def gather_last(buf, ss, rs, s):
        arrived(buf.at[s, 2], rs.at[s, 2])
        send(buf.at[s, 2], buf.at[s, 3], ss.at[24 + s], rs.at[s, 3], sibling)

    def gather_wait(buf, rs, s):
        arrived(buf.at[s, 1], rs.at[s, 1])
        arrived(buf.at[s, 3], rs.at[s, 3])

    gather_start(x_all, x_send, x_recv)

    w_low[144:LANES, :] = jnp.zeros((LANES - 144, w_low.shape[1]), BF16)
    copy_w.wait()
    w_low[0:classes, :] = w[...].astype(BF16)
    ro = readout_ref[...]
    ro_hi = ro.astype(BF16)
    rest = ro - ro_hi.astype(F32)
    ro_mid = rest.astype(BF16)
    ro_lo = (rest - ro_mid.astype(F32)).astype(BF16)
    nt = (((1,), (1,)), ((), ()))
    x0 = x_own[...]
    linear = (
        lax.dot_general(x0, ro_hi, nt, preferred_element_type=F32)
        + lax.dot_general(x0, ro_mid, nt, preferred_element_type=F32)
        + lax.dot_general(x0, ro_lo, nt, preferred_element_type=F32)
    )
    row = jnp.broadcast_to(labels_ref[pl.ds(z, 1), :].astype(F32), (128, 128))
    lab[...] = row.T
    copy_p.wait()

    turn = 1.0 / (2.0 * math.pi)
    scale = scale_ref[0] * turn

    def half(chunk, first):
        lo, hi = chunk
        n = (hi - lo) * 128
        xs = x_all[lo:hi].reshape(n, x_all.shape[-1])

        def block(j, carry):
            cols = pl.ds(pl.multiple_of(j * NB, NB), NB)
            product = jnp.dot(xs, proj[:, cols], preferred_element_type=F32)
            feats[lo * 128 : hi * 128, cols] = features_of(product, scale, shift_ref[:, cols] * turn)
            return carry

        count = feats.shape[1] // NB // 2
        lax.fori_loop(first * count, (first + 1) * count, block, 0, unroll=True)

    def scores(chunk):
        lo, hi = chunk
        part = lax.dot_general(feats[lo * 128 : hi * 128, :], w_low[...], nt, preferred_element_type=F32)
        part = part.reshape(hi - lo, 4, 32, LANES)
        for s in range(lo, hi):
            for j in range(2):
                kept[s, j] = part[s - lo, 2 * j]
                pair_out[s, j] = part[s - lo, 2 * j + 1].astype(BF16)
            send(pair_out.at[s], pair_in.at[s], pair_send.at[s], pair_recv.at[s], sibling)

    def pass_on(chunk):
        for s in range(*chunk):
            arrived(pair_in.at[s], pair_recv.at[s])
            m = MIRROR[s]
            for j in range(2):
                total = kept[s, j] + pair_in[s, j].astype(F32)
                if s == 0 and j == 0:
                    kept[0, 0] = total
                else:
                    sum_out[s, j] = total.astype(BF16)
                    dev = feat_dev(OFFS[s], q_x if j else q)
                    send(sum_out.at[s, j], sum_in.at[m, j], sum_send.at[s, j], sum_recv.at[m, j], dev)

    for index, chunk in enumerate(CHUNKS):
        later = CHUNKS[index + 1] if index + 1 < len(CHUNKS) else (0, 0)
        if index == 0:
            gather_last(x_all, x_send, x_recv, 0)
        for s in range(*later):
            gather_local(x_all, x_send, x_recv, s)
        for s in range(*chunk):
            gather_wait(x_all, x_recv, s)
        half(chunk, 0)
        for s in range(*later):
            gather_last(x_all, x_send, x_recv, s)
        if index:
            pass_on(CHUNKS[index - 1])
        half(chunk, 1)
        scores(chunk)
    pass_on(CHUNKS[-1])

    total = kept[0, 0]
    for s in range(8):
        for j in range(2):
            if s or j:
                arrived(sum_in.at[s, j], sum_recv.at[s, j])
                total = total + sum_in[s, j].astype(F32)
    lanes = lax.broadcasted_iota(jnp.int32, (32, LANES), 1)
    inside = lanes < classes
    linear = jnp.concatenate([linear, jnp.zeros((32, LANES - classes), F32)], axis=1)
    value = total * (1.0 / math.sqrt(feat_total)) + linear
    value = jnp.where(inside, value, -1e30)
    value = jnp.exp(value - jnp.max(value, axis=1, keepdims=True))
    probs = value / jnp.sum(value, axis=1, keepdims=True)
    mine = lab[pl.ds(pl.multiple_of(q * 32, 32), 32), :]
    mine = jnp.concatenate([mine, mine], axis=1)
    res_all[0, 0] = jnp.where(lanes.astype(F32) == mine, probs - 1.0, probs).astype(BF16)

    gather_start(res_all, res_send, res_recv)
    gather_last(res_all, res_send, res_recv, 0)
    for s in range(1, 8):
        gather_local(res_all, res_send, res_recv, s)
    for s in range(1, 8):
        gather_last(res_all, res_send, res_recv, s)
    for s in range(8):
        gather_wait(res_all, res_recv, s)

    res_t[...] = res_all[...].reshape(1024, LANES).T[:ROWS]
    cols_each = out_ref.shape[1]

    def grad_block(k):
        cols = pl.ds(pl.multiple_of(frame_dev(k) * cols_each, cols_each), cols_each)
        return jnp.dot(res_t[...], feats[:, cols], preferred_element_type=F32)

    back = [0] + [(k // 4) * 4 + (4 - k % 4) % 4 for k in range(1, 8)]
    for k in (6, 5, 7, 2, 4, 1, 3):
        grad_out[k] = grad_block(k).astype(BF16)
        b = back[k]
        send(grad_out.at[k], grad_in.at[b], grad_send.at[k], grad_recv.at[b], {"frames": frame_dev(k)})

    ro_grad = jnp.dot(res_t[...], x_all[...].reshape(1024, x_all.shape[-1]), preferred_element_type=F32)
    ro_t[...] = jnp.zeros_like(ro_t)
    ro_t[0 : ro_grad.shape[1], 0:ROWS] = ro_grad.T
    own_rows = pl.ds(pl.multiple_of(me * 16, 16), 16)
    ro_out[...] = ro_t[own_rows, :].astype(BF16)
    for k in range(1, 8):
        b = back[k]
        send(ro_out, ro_in.at[b], ro_send.at[k], ro_recv.at[b], {"frames": frame_dev(k)})
    own_grad = grad_block(0)
    total = ro_t[own_rows, :]
    for k in range(1, 8):
        arrived(ro_in.at[k], ro_recv.at[k])
        total = total + ro_in[k].astype(F32)
    ro_own[0, 0] = total.astype(BF16)
    gather_start(ro_own, all_send, all_recv)
    gather_last(ro_own, all_send, all_recv, 0)
    for s in range(1, 8):
        gather_local(ro_own, all_send, all_recv, s)
    for s in range(1, 8):
        gather_last(ro_own, all_send, all_recv, s)
    for s in range(8):
        gather_wait(ro_own, all_recv, s)
    for s in range(8):
        for r, qq in enumerate((q, q_sib, q_x, 3 - q)):
            at = (((z + OFFS[s] + 8) % 8) * 4 + qq) * 16
            grad_out_ref[pl.ds(pl.multiple_of(at, 16), 16), :] = ro_own[s, r].astype(F32)

    for k in range(1, 8):
        arrived(grad_in.at[k], grad_recv.at[k])
        own_grad = own_grad + grad_in[k].astype(F32)
    cols = pl.ds(pl.multiple_of(group * cols_each, cols_each), cols_each)
    stepped = w[:, cols] - (5.0 / math.sqrt(batch)) * own_grad[:classes]
    trimmed = stepped - jnp.clip(stepped, -1.0, 1.0)
    part = jnp.sum(trimmed * trimmed, axis=0, keepdims=True)
    norm_out[...] = jnp.broadcast_to(part, (8, cols_each))
    for k in range(1, 8):
        b = back[k]
        send(norm_out, norm_in.at[b], norm_send.at[k], norm_recv.at[b], {"frames": frame_dev(k)})
    for k in range(1, 8):
        arrived(norm_in.at[k], norm_recv.at[k])
        part = part + norm_in[k, 0:1, :]
    norm = jnp.sqrt(jnp.sum(part, axis=1, keepdims=True) + 1e-6)
    limit = 1.5 * math.sqrt(w.shape[0] * w.shape[1])
    out_ref[...] = trimmed * jnp.maximum(0.0, 1.0 - limit / norm)

    for copy in sends:
        copy.wait_send()


def body(frames_in, labels, projection, kernel_scale, shift, weights, readout):
    n_feat, n_frames = lax.axis_size("feat"), lax.axis_size("frames")
    rows, depth = frames_in.shape
    classes, columns = weights.shape
    batch = labels.shape[0] * n_frames
    each = columns // n_frames
    vmem = pl.BlockSpec(memory_space=pltpu.VMEM)
    hbm = pl.BlockSpec(memory_space=pl.ANY)
    dma = pltpu.SemaphoreType.DMA
    new_weights, ro_grad = pl.pallas_call(
        functools.partial(kernel, batch, columns * n_feat, classes),
        out_shape=(
            jax.ShapeDtypeStruct((classes, each), F32),
            jax.ShapeDtypeStruct((512, LANES), F32),
        ),
        in_specs=[pl.BlockSpec(memory_space=pltpu.SMEM), hbm, hbm, hbm, vmem, vmem, vmem],
        out_specs=(vmem, vmem),
        scratch_shapes=[
            pltpu.VMEM((rows, depth), BF16),
            pltpu.VMEM((depth, columns), BF16),
            pltpu.VMEM((classes, columns), F32),
            pltpu.VMEM((LANES, columns), BF16),
            pltpu.VMEM((8, 4, rows, depth), BF16),
            pltpu.VMEM((1024, columns), BF16),
            pltpu.VMEM((128, 128), F32),
            pltpu.VMEM((8, 2, rows, LANES), F32),
            pltpu.VMEM((8, 2, rows, LANES), BF16),
            pltpu.VMEM((8, 2, rows, LANES), BF16),
            pltpu.VMEM((8, 2, rows, LANES), BF16),
            pltpu.VMEM((8, 2, rows, LANES), BF16),
            pltpu.VMEM((8, 4, rows, LANES), BF16),
            pltpu.VMEM((ROWS, 1024), BF16),
            pltpu.VMEM((8, ROWS, each), BF16),
            pltpu.VMEM((8, ROWS, each), BF16),
            pltpu.VMEM((512, LANES), F32),
            pltpu.VMEM((16, LANES), BF16),
            pltpu.VMEM((8, 16, LANES), BF16),
            pltpu.VMEM((8, 4, 16, LANES), BF16),
            pltpu.VMEM((8, each), F32),
            pltpu.VMEM((8, 8, each), F32),
            dma((3,)),
            dma((32,)), dma((8, 4)),
            dma((8,)), dma((8,)),
            dma((8, 2)), dma((8, 2)),
            dma((32,)), dma((8, 4)),
            dma((8,)), dma((8,)),
            dma((8,)), dma((8,)),
            dma((32,)), dma((8, 4)),
            dma((8,)), dma((8,)),
        ],
        compiler_params=pltpu.CompilerParams(
            collective_id=0, has_side_effects=True, vmem_limit_bytes=56 * 2**20
        ),
        name="fourier_step",
    )(kernel_scale, frames_in, projection, weights, labels.reshape(8, 128), shift.reshape(1, -1), readout)
    new_readout = readout - 3.0 / math.sqrt(batch) * ro_grad[:depth, :classes].T
    return (new_weights, new_readout)


def solution(mesh):
    return jax.shard_map(
        body,
        mesh=mesh,
        in_specs=(
            P(("frames", "feat"), None),
            P("frames"),
            P(None, "feat"),
            P("feat"),
            P("feat"),
            P(None, "feat"),
            P(),
        ),
        out_specs=(P(None, ("feat", "frames")), P()),
        check_vma=False,
    )
```

```python
import functools
import math

import jax
import jax.numpy as jnp
from jax import lax
from jax.experimental import pallas as pl
from jax.experimental.pallas import tpu as pltpu
from jax.sharding import PartitionSpec as P

MESH = pl.DeviceIdType.MESH
F32, BF16 = jnp.float32, jnp.bfloat16
ROWS = 160
NB = 256

OFFS = (0, 1, -1, 2, -2, 3, -3, 4)
MIRROR = tuple(OFFS.index(-d) if -d in OFFS else OFFS.index(d) for d in OFFS)
CHUNKS = ((0, 1), (1, 3), (3, 5), (5, 7), (7, 8))

COS = (1.4142124652862549, -27.91513442993164, 91.82299041748047, -120.59228515625, 83.1423110961914, -29.799043655395508)


def features_of(product, scale, shift):
    turns = product * scale + shift
    r = turns - jnp.round(turns)
    u = r * r
    acc = COS[-1] * u + COS[-2]
    for c in COS[-3::-1]:
        acc = acc * u + c
    return acc.astype(BF16)


def kernel(
    batch, feat_total, classes,
    scale_ref, x_hbm, proj_hbm, w_hbm, labels_hbm, shift_hbm, readout_hbm,
    out_ref, factor_ref, readout_out_ref,
    x_own, proj, w, labels, shift, readout, w_low, x_all, feats, sum_out, sum_in, loc, res_all, res_t,
    grad_out, grad_in, ro_pad, ro_out, ro_in, ro_all, norm_out, norm_in,
    local_sem, x_send, x_recv, sum_send, sum_recv, loc_send, loc_recv, res_send, res_recv, res_pass, res_got,
    grad_send, grad_recv, ro_send, ro_recv, all_send, all_recv, norm_send, norm_recv,
):
    me = lax.axis_index("feat")
    group = lax.axis_index("frames")
    z, q = me // 4, me % 4
    xh, y = group // 4, group % 4
    core = q % 2
    q_sib = q + 1 - 2 * core
    q_x = (q + 2) % 4

    def feat_dev(d, qq):
        return {"feat": ((z + d + 8) % 8) * 4 + qq}

    def frame_dev(k):
        dx, dy = k // 4, k % 4
        return ((xh + dx) % 2) * 4 + (y + dy) % 4

    sibling, neighbour, across = feat_dev(0, q_sib), feat_dev(0, q_x), feat_dev(0, 3 - q)
    sends = []

    def send(src, dst, ssem, rsem, dev):
        copy = pltpu.make_async_remote_copy(
            src_ref=src, dst_ref=dst, send_sem=ssem, recv_sem=rsem, device_id=dev, device_id_type=MESH
        )
        copy.start()
        sends.append(copy)

    def arrived(ref, rsem):
        pltpu.make_async_remote_copy(
            src_ref=ref, dst_ref=ref, send_sem=x_send.at[0], recv_sem=rsem, device_id=sibling, device_id_type=MESH
        ).wait_recv()

    local = [
        pltpu.make_async_copy(src, dst, local_sem.at[i])
        for i, (src, dst) in enumerate(
            ((x_hbm, x_own), (shift_hbm, shift), (proj_hbm, proj), (w_hbm, w), (labels_hbm, labels), (readout_hbm, readout))
        )
    ]
    for copy in local:
        copy.start()

    barrier = pltpu.get_barrier_semaphore()
    partners = [feat_dev(d, q) for d in OFFS[1:]] + [neighbour, across, sibling]
    partners += [{"frames": frame_dev(k)} for k in range(1, 8)]
    for dev in partners:
        pl.semaphore_signal(barrier, inc=1, device_id=dev, device_id_type=MESH)
    local[0].wait()
    x_all[0, q] = x_own[...]
    pl.semaphore_wait(barrier, len(partners))

    def gather_start(buf, ss, rs, at, at_mirror):
        gather_local(buf, ss, rs, at, 0, False)
        for s in range(1, 8):
            m = MIRROR[s]
            send(buf.at[at(0), q], buf.at[at_mirror(m), q], ss.at[s], rs.at[m, 0], feat_dev(OFFS[s], q))

    def gather_local(buf, ss, rs, at, s, wait=True):
        piece = buf.at[at(s), q]
        if wait:
            arrived(piece, rs.at[s, 0])
        send(piece, piece, ss.at[8 + s], rs.at[s, 2], neighbour)
        send(piece, piece, ss.at[16 + s], rs.at[s, 1], sibling)

    def gather_last(buf, ss, rs, at, s):
        piece = buf.at[at(s), q_x]
        arrived(piece, rs.at[s, 2])
        send(piece, piece, ss.at[24 + s], rs.at[s, 3], sibling)

    def gather_wait(buf, rs, at, s):
        arrived(buf.at[at(s), q_sib], rs.at[s, 1])
        arrived(buf.at[at(s), 3 - q], rs.at[s, 3])

    def relative(s):
        return s

    def x_local(*slots):
        for s in slots:
            gather_local(x_all, x_send, x_recv, relative, s)

    def x_last(*slots):
        for s in slots:
            gather_last(x_all, x_send, x_recv, relative, s)

    def x_wait(*slots):
        for s in slots:
            gather_wait(x_all, x_recv, relative, s)

    gather_start(x_all, x_send, x_recv, relative, relative)

    w_low[144:ROWS, :] = jnp.zeros((ROWS - 144, w_low.shape[1]), BF16)
    local[3].wait()
    w_low[0:classes, :] = w[...].astype(BF16)
    local[1].wait()
    local[2].wait()

    nt = (((1,), (1,)), ((), ()))
    turn = 1.0 / (2.0 * math.pi)
    scale = scale_ref[0] * turn

    def half(chunk, first):
        lo, hi = CHUNKS[chunk]
        n = (hi - lo) * 128
        xs = x_all[lo:hi].reshape(n, x_all.shape[-1])

        def block(j, carry):
            cols = pl.ds(pl.multiple_of(j * NB, NB), NB)
            product = jnp.dot(xs, proj[:, cols], preferred_element_type=F32)
            feats[lo * 128 : hi * 128, cols] = features_of(product, scale, shift[:, cols] * turn)
            return carry

        count = feats.shape[1] // NB // 2
        lax.fori_loop(first * count, (first + 1) * count, block, 0, unroll=True)

    def scores(chunk):
        lo, hi = CHUNKS[chunk]
        part = lax.dot_general(w_low[...], feats[lo * 128 : hi * 128, :], nt, preferred_element_type=F32)
        for s in range(lo, hi):
            if s == 0:
                return part
            m = MIRROR[s]
            sum_out[s] = part[:, (s - lo) * 128 : (s - lo + 1) * 128].astype(BF16)
            send(sum_out.at[s], sum_in.at[m], sum_send.at[s], sum_recv.at[m], feat_dev(OFFS[s], q))

    x_last(0)
    x_local(1, 2)
    x_wait(0)
    half(0, 0)
    x_local(3, 4)
    x_last(1, 2)
    half(0, 1)
    total = scores(0)
    x_wait(1, 2)
    half(1, 0)
    x_local(5, 6)
    x_last(3, 4)
    half(1, 1)
    scores(1)
    x_wait(3, 4)
    x_local(7)
    half(2, 0)
    x_last(5, 6)
    half(2, 1)
    scores(2)
    x_wait(5, 6)
    half(3, 0)
    x_last(7)
    half(3, 1)
    scores(3)
    x_wait(7)
    half(4, 0)
    half(4, 1)
    scores(4)

    local[4].wait()
    local[5].wait()
    ro = readout[...]
    ro_hi = ro.astype(BF16)
    rest = ro - ro_hi.astype(F32)
    ro_mid = rest.astype(BF16)
    ro_lo = (rest - ro_mid.astype(F32)).astype(BF16)
    x0 = x_all[0].reshape(128, x_all.shape[-1])
    linear = (
        lax.dot_general(ro_hi, x0, nt, preferred_element_type=F32)
        + lax.dot_general(ro_mid, x0, nt, preferred_element_type=F32)
        + lax.dot_general(ro_lo, x0, nt, preferred_element_type=F32)
    )
    linear = jnp.concatenate([linear, jnp.zeros((ROWS - classes, 128), F32)], axis=0)

    for s in range(1, 8):
        arrived(sum_in.at[s], sum_recv.at[s])
        total = total + sum_in[s].astype(F32)
    loc[q] = total.astype(BF16)
    mine = loc.at[q]
    send(mine, mine, loc_send.at[2], loc_recv.at[2], neighbour)
    send(mine, mine, loc_send.at[3], loc_recv.at[3], across)
    send(mine, mine, loc_send.at[1], loc_recv.at[1], sibling)
    arrived(loc.at[q_sib], loc_recv.at[1])
    arrived(loc.at[q_x], loc_recv.at[2])
    arrived(loc.at[3 - q], loc_recv.at[3])
    total = loc[0].astype(F32)
    for k in range(1, 4):
        total = total + loc[k].astype(F32)
    rows = lax.broadcasted_iota(jnp.int32, (ROWS, 128), 0)
    inside = rows < classes
    value = jnp.where(inside, total * (1.0 / math.sqrt(feat_total)) + linear, -1e30)
    value = jnp.exp(value - jnp.max(value, axis=0, keepdims=True))
    probs = value / jnp.sum(value, axis=0, keepdims=True)
    label = labels[pl.ds(z, 1), :]
    residual = jnp.where(rows == label, probs - 1.0, probs)
    res_all[0] = residual.astype(BF16).reshape(2, ROWS // 2, 128)

    for s in range(1, 8):
        m = MIRROR[s]
        send(res_all.at[0, core], res_all.at[m, core], res_send.at[s], res_recv.at[m], feat_dev(OFFS[s], q))
    for s in range(1, 8):
        piece = res_all.at[s, core]
        arrived(piece, res_recv.at[s])
        send(piece, piece, res_pass.at[s], res_got.at[s], sibling)
    for s in range(8):
        if s:
            arrived(res_all.at[s, 1 - core], res_got.at[s])
        res_t[:, s * 128 : (s + 1) * 128] = res_all[s].reshape(ROWS, 128)

    cols_each = out_ref.shape[1]

    def grad_block(k):
        cols = pl.ds(pl.multiple_of(frame_dev(k) * cols_each, cols_each), cols_each)
        return jnp.dot(res_t[...], feats[:, cols], preferred_element_type=F32)

    back = [0] + [(k // 4) * 4 + (4 - k % 4) % 4 for k in range(1, 8)]

    def grad_send_block(k):
        grad_out[k] = grad_block(k).astype(BF16)
        b = back[k]
        send(grad_out.at[k], grad_in.at[b], grad_send.at[k], grad_recv.at[b], {"frames": frame_dev(k)})

    grad_send_block(6)

    ro_pad[...] = jnp.zeros_like(ro_pad)
    depth = x_all.shape[-1]
    ro_pad[0:ROWS, 0:depth] = jnp.dot(res_t[...], x_all[...].reshape(1024, depth), preferred_element_type=F32)
    ro_mine = ro_pad[pl.ds(pl.multiple_of(z * 32, 32), 32), pl.ds(pl.multiple_of(q * 128, 128), 128)]
    ro_out[...] = ro_mine.astype(BF16)
    for k in range(1, 8):
        b = back[k]
        send(ro_out, ro_in.at[b], ro_send.at[k], ro_recv.at[b], {"frames": frame_dev(k)})

    for k in (5, 7, 2, 4, 1, 3):
        grad_send_block(k)
    own_grad = grad_block(0)

    def absolute(s):
        return (z + OFFS[s] + 8) % 8

    def mine_at(m):
        return z

    for k in range(1, 8):
        arrived(ro_in.at[k], ro_recv.at[k])
        ro_mine = ro_mine + ro_in[k].astype(F32)
    ro_all[z, q] = ro_mine.astype(BF16)
    gather_start(ro_all, all_send, all_recv, absolute, mine_at)
    gather_last(ro_all, all_send, all_recv, absolute, 0)
    for s in range(1, 8):
        gather_local(ro_all, all_send, all_recv, absolute, s)
    for s in range(1, 8):
        gather_last(ro_all, all_send, all_recv, absolute, s)
    for s in range(8):
        gather_wait(ro_all, all_recv, absolute, s)
    for i in range(0, classes, 32):
        n = min(32, classes - i)
        grad = jnp.concatenate([ro_all[i // 32, k] for k in range(4)], axis=1).astype(F32)
        readout_out_ref[i : i + n, :] = ro[i : i + n] - (3.0 / math.sqrt(batch)) * grad[:n, :depth]

    for k in (3, 1, 4, 2, 7, 5, 6):
        arrived(grad_in.at[k], grad_recv.at[k])
        own_grad = own_grad + grad_in[k].astype(F32)
    cols = pl.ds(pl.multiple_of(group * cols_each, cols_each), cols_each)
    stepped = w[:, cols] - (5.0 / math.sqrt(batch)) * own_grad[:classes]
    trimmed = stepped - jnp.clip(stepped, -1.0, 1.0)
    part = jnp.sum(trimmed * trimmed, axis=0, keepdims=True)
    part = part[:, 0:128] + part[:, 128:256] + part[:, 256:384] + part[:, 384:512]
    norm_out[...] = jnp.broadcast_to(part, (8, 128))
    for k in range(1, 8):
        b = back[k]
        send(norm_out, norm_in.at[b], norm_send.at[k], norm_recv.at[b], {"frames": frame_dev(k)})
    out_ref[...] = trimmed
    for k in range(1, 8):
        arrived(norm_in.at[k], norm_recv.at[k])
        part = part + norm_in[k, 0:1, :]
    norm = jnp.sqrt(jnp.sum(part, axis=1, keepdims=True) + 1e-6)
    limit = 1.5 * math.sqrt(w.shape[0] * w.shape[1])
    factor_ref[...] = jnp.broadcast_to(jnp.maximum(0.0, 1.0 - limit / norm), (8, 128))

    for copy in sends:
        copy.wait_send()


def body(frames_in, labels, projection, kernel_scale, shift, weights, readout):
    n_feat, n_frames = lax.axis_size("feat"), lax.axis_size("frames")
    rows, depth = frames_in.shape
    classes, columns = weights.shape
    batch = labels.shape[0] * n_frames
    each = columns // n_frames
    vmem = pl.BlockSpec(memory_space=pltpu.VMEM)
    hbm = pl.BlockSpec(memory_space=pl.ANY)
    dma = pltpu.SemaphoreType.DMA
    trimmed, factor, new_readout = pl.pallas_call(
        functools.partial(kernel, batch, columns * n_feat, classes),
        out_shape=(
            jax.ShapeDtypeStruct((classes, each), F32),
            jax.ShapeDtypeStruct((8, 128), F32),
            jax.ShapeDtypeStruct(readout.shape, F32),
        ),
        in_specs=[pl.BlockSpec(memory_space=pltpu.SMEM)] + [hbm] * 6,
        out_specs=(vmem, vmem, vmem),
        scratch_shapes=[
            pltpu.VMEM((rows, depth), BF16),
            pltpu.VMEM((depth, columns), BF16),
            pltpu.VMEM((classes, columns), F32),
            pltpu.VMEM((8, 128), jnp.int32),
            pltpu.VMEM((1, columns), F32),
            pltpu.VMEM(readout.shape, F32),
            pltpu.VMEM((ROWS, columns), BF16),
            pltpu.VMEM((8, 4, rows, depth), BF16),
            pltpu.VMEM((1024, columns), BF16),
            pltpu.VMEM((8, ROWS, 128), BF16),
            pltpu.VMEM((8, ROWS, 128), BF16),
            pltpu.VMEM((4, ROWS, 128), BF16),
            pltpu.VMEM((8, 2, ROWS // 2, 128), BF16),
            pltpu.VMEM((ROWS, 1024), BF16),
            pltpu.VMEM((8, ROWS, each), BF16),
            pltpu.VMEM((8, ROWS, each), BF16),
            pltpu.VMEM((256, 512), F32),
            pltpu.VMEM((32, 128), BF16),
            pltpu.VMEM((8, 32, 128), BF16),
            pltpu.VMEM((8, 4, 32, 128), BF16),
            pltpu.VMEM((8, 128), F32),
            pltpu.VMEM((8, 8, 128), F32),
            dma((6,)),
            dma((32,)), dma((8, 4)),
            dma((8,)), dma((8,)),
            dma((4,)), dma((4,)),
            dma((8,)), dma((8,)), dma((8,)), dma((8,)),
            dma((8,)), dma((8,)),
            dma((8,)), dma((8,)),
            dma((32,)), dma((8, 4)),
            dma((8,)), dma((8,)),
        ],
        compiler_params=pltpu.CompilerParams(
            collective_id=0, has_side_effects=True, vmem_limit_bytes=56 * 2**20
        ),
        name="fourier_step",
    )(kernel_scale, frames_in, projection, weights, labels.reshape(8, 128), shift.reshape(1, -1), readout)
    return (trimmed * factor[0, 0], new_readout)


def solution(mesh):
    return jax.shard_map(
        body,
        mesh=mesh,
        in_specs=(
            P(("frames", "feat"), None),
            P("frames"),
            P(None, "feat"),
            P("feat"),
            P("feat"),
            P(None, "feat"),
            P(),
        ),
        out_specs=(P(None, ("feat", "frames")), P()),
        check_vma=False,
    )
```

```python
import functools
import math

import jax
import jax.numpy as jnp
from jax import lax
from jax.experimental import pallas as pl
from jax.experimental.pallas import tpu as pltpu
from jax.sharding import PartitionSpec as P

MESH = pl.DeviceIdType.MESH
F32, BF16 = jnp.float32, jnp.bfloat16
ROWS = 160
NB = 256

OFFS = (0, 1, -1, 2, -2, 3, -3, 4)
MIRROR = tuple(OFFS.index(-d) if -d in OFFS else OFFS.index(d) for d in OFFS)
CHUNKS = ((0, 1), (1, 3), (3, 5), (5, 7), (7, 8))

COS = (1.4142124652862549, -27.91513442993164, 91.82299041748047, -120.59228515625, 83.1423110961914, -29.799043655395508)


def features_of(product, scale, shift):
    turns = product * scale + shift
    r = turns - jnp.round(turns)
    u = r * r
    acc = COS[-1] * u + COS[-2]
    for c in COS[-3::-1]:
        acc = acc * u + c
    return acc.astype(BF16)


def kernel(
    batch, feat_total, classes,
    scale_ref, x_hbm, proj_hbm, w_hbm, labels_hbm, shift_hbm, readout_hbm,
    out_ref, readout_out_ref,
    x_own, proj, w, labels, shift, readout, w_low, x_all, feats, sum_out, sum_in, loc, res_all, res_t,
    grad_out, grad_in, ro_pad, ro_out, ro_in, ro_all, norm_out, norm_in,
    local_sem, x_send, x_recv, sum_send, sum_recv, loc_send, loc_recv, res_send, res_recv, res_pass, res_got,
    grad_send, grad_recv, ro_send, ro_recv, all_send, all_recv, all_pass, all_got, norm_send, norm_recv,
):
    me = lax.axis_index("feat")
    group = lax.axis_index("frames")
    z, q = me // 4, me % 4
    xh, y = group // 4, group % 4
    core = q % 2
    q_sib = q + 1 - 2 * core
    q_x = (q + 2) % 4

    def feat_dev(d, qq):
        return {"feat": ((z + d + 8) % 8) * 4 + qq}

    def frame_dev(k):
        dx, dy = k // 4, k % 4
        return ((xh + dx) % 2) * 4 + (y + dy) % 4

    sibling, neighbour, across = feat_dev(0, q_sib), feat_dev(0, q_x), feat_dev(0, 3 - q)
    sends = []

    def send(src, dst, ssem, rsem, dev):
        copy = pltpu.make_async_remote_copy(
            src_ref=src, dst_ref=dst, send_sem=ssem, recv_sem=rsem, device_id=dev, device_id_type=MESH
        )
        copy.start()
        sends.append(copy)

    def arrived(ref, rsem):
        pltpu.make_async_remote_copy(
            src_ref=ref, dst_ref=ref, send_sem=x_send.at[0], recv_sem=rsem, device_id=sibling, device_id_type=MESH
        ).wait_recv()

    local = [
        pltpu.make_async_copy(src, dst, local_sem.at[i])
        for i, (src, dst) in enumerate(
            ((x_hbm, x_own), (shift_hbm, shift), (proj_hbm, proj), (w_hbm, w), (labels_hbm, labels), (readout_hbm, readout))
        )
    ]
    for copy in local:
        copy.start()

    barrier = pltpu.get_barrier_semaphore()
    partners = [feat_dev(d, q) for d in OFFS[1:]] + [neighbour, across, sibling]
    partners += [{"frames": frame_dev(k)} for k in range(1, 8)]
    for dev in partners:
        pl.semaphore_signal(barrier, inc=1, device_id=dev, device_id_type=MESH)
    local[0].wait()
    x_all[0, q] = x_own[...]
    pl.semaphore_wait(barrier, len(partners))

    def gather_start(buf, ss, rs, at, at_mirror):
        gather_local(buf, ss, rs, at, 0, False)
        for s in range(1, 8):
            m = MIRROR[s]
            send(buf.at[at(0), q], buf.at[at_mirror(m), q], ss.at[s], rs.at[m, 0], feat_dev(OFFS[s], q))

    def gather_local(buf, ss, rs, at, s, wait=True):
        piece = buf.at[at(s), q]
        if wait:
            arrived(piece, rs.at[s, 0])
        send(piece, piece, ss.at[8 + s], rs.at[s, 2], neighbour)
        send(piece, piece, ss.at[16 + s], rs.at[s, 1], sibling)

    def gather_last(buf, ss, rs, at, s):
        piece = buf.at[at(s), q_x]
        arrived(piece, rs.at[s, 2])
        send(piece, piece, ss.at[24 + s], rs.at[s, 3], sibling)

    def gather_wait(buf, rs, at, s):
        arrived(buf.at[at(s), q_sib], rs.at[s, 1])
        arrived(buf.at[at(s), 3 - q], rs.at[s, 3])

    def relative(s):
        return s

    def x_local(*slots):
        for s in slots:
            gather_local(x_all, x_send, x_recv, relative, s)

    def x_last(*slots):
        for s in slots:
            gather_last(x_all, x_send, x_recv, relative, s)

    def x_wait(*slots):
        for s in slots:
            gather_wait(x_all, x_recv, relative, s)

    gather_start(x_all, x_send, x_recv, relative, relative)

    w_low[144:ROWS, :] = jnp.zeros((ROWS - 144, w_low.shape[1]), BF16)
    local[3].wait()
    w_low[0:classes, :] = w[...].astype(BF16)
    local[1].wait()
    local[2].wait()

    nt = (((1,), (1,)), ((), ()))
    turn = 1.0 / (2.0 * math.pi)
    scale = scale_ref[0] * turn

    def half(chunk, first):
        lo, hi = CHUNKS[chunk]
        n = (hi - lo) * 128
        xs = x_all[lo:hi].reshape(n, x_all.shape[-1])

        def block(j, carry):
            cols = pl.ds(pl.multiple_of(j * NB, NB), NB)
            product = jnp.dot(xs, proj[:, cols], preferred_element_type=F32)
            feats[lo * 128 : hi * 128, cols] = features_of(product, scale, shift[:, cols] * turn)
            return carry

        count = feats.shape[1] // NB // 2
        lax.fori_loop(first * count, (first + 1) * count, block, 0, unroll=True)

    def scores(chunk):
        lo, hi = CHUNKS[chunk]
        part = lax.dot_general(w_low[...], feats[lo * 128 : hi * 128, :], nt, preferred_element_type=F32)
        for s in range(lo, hi):
            if s == 0:
                return part
            m = MIRROR[s]
            sum_out[s] = part[:, (s - lo) * 128 : (s - lo + 1) * 128].astype(BF16)
            send(sum_out.at[s], sum_in.at[m], sum_send.at[s], sum_recv.at[m], feat_dev(OFFS[s], q))

    x_last(0)
    x_local(1, 2)
    x_wait(0)
    half(0, 0)
    x_local(3, 4)
    x_last(1, 2)
    half(0, 1)
    total = scores(0)
    x_local(5, 6)
    x_last(3, 4)
    x_wait(1, 2)
    half(1, 0)
    x_local(7)
    half(1, 1)
    scores(1)
    x_last(5, 6)
    x_wait(3, 4)
    half(2, 0)
    x_last(7)
    half(2, 1)
    scores(2)
    x_wait(5, 6)
    half(3, 0)
    half(3, 1)
    scores(3)
    x_wait(7)
    half(4, 0)
    half(4, 1)
    scores(4)

    local[4].wait()
    local[5].wait()
    ro = readout[...]
    ro_hi = ro.astype(BF16)
    rest = ro - ro_hi.astype(F32)
    ro_mid = rest.astype(BF16)
    ro_lo = (rest - ro_mid.astype(F32)).astype(BF16)
    x0 = x_all[0].reshape(128, x_all.shape[-1])
    linear = (
        lax.dot_general(ro_hi, x0, nt, preferred_element_type=F32)
        + lax.dot_general(ro_mid, x0, nt, preferred_element_type=F32)
        + lax.dot_general(ro_lo, x0, nt, preferred_element_type=F32)
    )
    linear = jnp.concatenate([linear, jnp.zeros((ROWS - classes, 128), F32)], axis=0)

    for s in range(1, 8):
        arrived(sum_in.at[s], sum_recv.at[s])
        total = total + sum_in[s].astype(F32)
    loc[q] = total.astype(BF16)
    mine = loc.at[q]
    send(mine, mine, loc_send.at[2], loc_recv.at[2], neighbour)
    send(mine, mine, loc_send.at[3], loc_recv.at[3], across)
    send(mine, mine, loc_send.at[1], loc_recv.at[1], sibling)
    arrived(loc.at[q_sib], loc_recv.at[1])
    arrived(loc.at[q_x], loc_recv.at[2])
    arrived(loc.at[3 - q], loc_recv.at[3])
    total = loc[0].astype(F32)
    for k in range(1, 4):
        total = total + loc[k].astype(F32)
    rows = lax.broadcasted_iota(jnp.int32, (ROWS, 128), 0)
    inside = rows < classes
    value = jnp.where(inside, total * (1.0 / math.sqrt(feat_total)) + linear, -1e30)
    value = jnp.exp(value - jnp.max(value, axis=0, keepdims=True))
    probs = value / jnp.sum(value, axis=0, keepdims=True)
    label = labels[pl.ds(z, 1), :]
    residual = jnp.where(rows == label, probs - 1.0, probs)
    res_all[0] = residual.astype(BF16).reshape(2, ROWS // 2, 128)

    for s in range(1, 8):
        m = MIRROR[s]
        send(res_all.at[0, core], res_all.at[m, core], res_send.at[s], res_recv.at[m], feat_dev(OFFS[s], q))
    for s in range(1, 8):
        piece = res_all.at[s, core]
        arrived(piece, res_recv.at[s])
        send(piece, piece, res_pass.at[s], res_got.at[s], sibling)
    for s in range(8):
        if s:
            arrived(res_all.at[s, 1 - core], res_got.at[s])
        res_t[:, s * 128 : (s + 1) * 128] = res_all[s].reshape(ROWS, 128)

    cols_each = out_ref.shape[1]

    def grad_block(k):
        cols = pl.ds(pl.multiple_of(frame_dev(k) * cols_each, cols_each), cols_each)
        return jnp.dot(res_t[...], feats[:, cols], preferred_element_type=F32)

    back = [0] + [(k // 4) * 4 + (4 - k % 4) % 4 for k in range(1, 8)]

    def grad_send_block(k):
        grad_out[k] = grad_block(k).astype(BF16)
        b = back[k]
        send(grad_out.at[k], grad_in.at[b], grad_send.at[k], grad_recv.at[b], {"frames": frame_dev(k)})

    grad_send_block(6)

    ro_pad[...] = jnp.zeros_like(ro_pad)
    depth = x_all.shape[-1]
    ro_pad[0:ROWS, 0:depth] = jnp.dot(res_t[...], x_all[...].reshape(1024, depth), preferred_element_type=F32)
    ro_mine = ro_pad[pl.ds(pl.multiple_of(z * 32, 32), 32), pl.ds(pl.multiple_of(core * 256, 256), 256)]
    ro_out[...] = ro_mine.astype(BF16)
    for k in range(1, 8):
        b = back[k]
        send(ro_out, ro_in.at[b], ro_send.at[k], ro_recv.at[b], {"frames": frame_dev(k)})

    for k in (5, 7, 2, 4, 1, 3):
        grad_send_block(k)
    own_grad = grad_block(0)

    for k in range(1, 8):
        arrived(ro_in.at[k], ro_recv.at[k])
        ro_mine = ro_mine + ro_in[k].astype(F32)
    ro_all[z, core] = ro_mine.astype(BF16)
    mine = ro_all.at[z, core]
    for s in range(1, 8):
        send(mine, mine, all_send.at[s], all_recv.at[MIRROR[s]], feat_dev(OFFS[s], q))
    send(mine, mine, all_pass.at[0], all_got.at[0], sibling)
    for s in range(1, 8):
        piece = ro_all.at[(z + OFFS[s] + 8) % 8, core]
        arrived(piece, all_recv.at[s])
        send(piece, piece, all_pass.at[s], all_got.at[s], sibling)

    for k in (3, 1, 4, 2, 7, 5, 6):
        arrived(grad_in.at[k], grad_recv.at[k])
        own_grad = own_grad + grad_in[k].astype(F32)
    cols = pl.ds(pl.multiple_of(group * cols_each, cols_each), cols_each)
    stepped = w[:, cols] - (5.0 / math.sqrt(batch)) * own_grad[:classes]
    trimmed = stepped - jnp.clip(stepped, -1.0, 1.0)
    part = jnp.sum(trimmed * trimmed, axis=0, keepdims=True)
    part = part[:, 0:128] + part[:, 128:256] + part[:, 256:384] + part[:, 384:512]
    norm_out[...] = jnp.broadcast_to(part, (8, 128))
    for k in range(1, 8):
        b = back[k]
        send(norm_out, norm_in.at[b], norm_send.at[k], norm_recv.at[b], {"frames": frame_dev(k)})
    for s in range(8):
        arrived(ro_all.at[(z + OFFS[s] + 8) % 8, 1 - core], all_got.at[s])
    for i in range(0, classes, 32):
        n = min(32, classes - i)
        grad = jnp.concatenate([ro_all[i // 32, k] for k in range(2)], axis=1).astype(F32)
        readout_out_ref[i : i + n, :] = ro[i : i + n] - (3.0 / math.sqrt(batch)) * grad[:n, :depth]
    for k in range(1, 8):
        arrived(norm_in.at[k], norm_recv.at[k])
        part = part + norm_in[k, 0:1, :]
    norm = jnp.sqrt(jnp.sum(part, axis=1, keepdims=True) + 1e-6)
    limit = 1.5 * math.sqrt(w.shape[0] * w.shape[1])
    out_ref[...] = trimmed * jnp.maximum(0.0, 1.0 - limit / norm)

    for copy in sends:
        copy.wait_send()


def body(frames_in, labels, projection, kernel_scale, shift, weights, readout):
    n_feat, n_frames = lax.axis_size("feat"), lax.axis_size("frames")
    rows, depth = frames_in.shape
    classes, columns = weights.shape
    batch = labels.shape[0] * n_frames
    each = columns // n_frames
    vmem = pl.BlockSpec(memory_space=pltpu.VMEM)
    hbm = pl.BlockSpec(memory_space=pl.ANY)
    dma = pltpu.SemaphoreType.DMA
    return pl.pallas_call(
        functools.partial(kernel, batch, columns * n_feat, classes),
        out_shape=(
            pltpu.VMEM((classes, each), F32),
            pltpu.VMEM(readout.shape, F32),
        ),
        in_specs=[pl.BlockSpec(memory_space=pltpu.SMEM)] + [hbm] * 6,
        out_specs=(vmem, vmem),
        scratch_shapes=[
            pltpu.VMEM((rows, depth), BF16),
            pltpu.VMEM((depth, columns), BF16),
            pltpu.VMEM((classes, columns), F32),
            pltpu.VMEM((8, 128), jnp.int32),
            pltpu.VMEM((1, columns), F32),
            pltpu.VMEM(readout.shape, F32),
            pltpu.VMEM((ROWS, columns), BF16),
            pltpu.VMEM((8, 4, rows, depth), BF16),
            pltpu.VMEM((1024, columns), BF16),
            pltpu.VMEM((8, ROWS, 128), BF16),
            pltpu.VMEM((8, ROWS, 128), BF16),
            pltpu.VMEM((4, ROWS, 128), BF16),
            pltpu.VMEM((8, 2, ROWS // 2, 128), BF16),
            pltpu.VMEM((ROWS, 1024), BF16),
            pltpu.VMEM((8, ROWS, each), BF16),
            pltpu.VMEM((8, ROWS, each), BF16),
            pltpu.VMEM((256, 512), F32),
            pltpu.VMEM((32, 256), BF16),
            pltpu.VMEM((8, 32, 256), BF16),
            pltpu.VMEM((8, 2, 32, 256), BF16),
            pltpu.VMEM((8, 128), F32),
            pltpu.VMEM((8, 8, 128), F32),
            dma((6,)),
            dma((32,)), dma((8, 4)),
            dma((8,)), dma((8,)),
            dma((4,)), dma((4,)),
            dma((8,)), dma((8,)), dma((8,)), dma((8,)),
            dma((8,)), dma((8,)),
            dma((8,)), dma((8,)),
            dma((8,)), dma((8,)), dma((8,)), dma((8,)),
            dma((8,)), dma((8,)),
        ],
        compiler_params=pltpu.CompilerParams(
            collective_id=0, has_side_effects=True, vmem_limit_bytes=56 * 2**20
        ),
        name="fourier_step",
    )(kernel_scale, frames_in, projection, weights, labels.reshape(8, 128), shift.reshape(1, -1), readout)


def solution(mesh):
    return jax.shard_map(
        body,
        mesh=mesh,
        in_specs=(
            P(("frames", "feat"), None),
            P("frames"),
            P(None, "feat"),
            P("feat"),
            P("feat"),
            P(None, "feat"),
            P(),
        ),
        out_specs=(P(None, ("feat", "frames")), P()),
        check_vma=False,
    )
```

```python
import functools
import math

import jax
import jax.numpy as jnp
from jax import lax
from jax.experimental import pallas as pl
from jax.experimental.pallas import tpu as pltpu
from jax.sharding import PartitionSpec as P

MESH = pl.DeviceIdType.MESH
F32, BF16 = jnp.float32, jnp.bfloat16
ROWS = 160
NB = 256
XF = 256

OFFS = (0, 1, -1, 2, -2, 3, -3, 4)
MIRROR = tuple(OFFS.index(-d) if -d in OFFS else OFFS.index(d) for d in OFFS)
CHUNKS = ((0, 1), (1, 3), (3, 5), (5, 7), (7, 8))

COS = (1.4142124652862549, -27.91513442993164, 91.82299041748047, -120.59228515625, 83.1423110961914, -29.799043655395508)


def features_of(product, scale, shift):
    turns = product * scale + shift
    r = turns - jnp.round(turns)
    u = r * r
    acc = COS[-1] * u + COS[-2]
    for c in COS[-3::-1]:
        acc = acc * u + c
    return acc.astype(BF16)


def kernel(
    batch, feat_total, classes,
    scale_ref, x_hbm, proj_hbm, w_hbm, labels_hbm, shift_hbm, readout_hbm,
    out_ref, readout_out_ref,
    proj, w, labels, shift, readout, w_low, x_all, feats, kept, pair_out, pair_in, sum_out, sum_in, loc, final, res_all, res_t,
    gx_out, gx_in, gy_out, gy_in, cy_out, cy_in, cx, kx, ky, ro_pad, ro_out, ro_in, ro_all, norm_out, norm_in,
    local_sem, x_send, x_recv, pair_send, pair_recv, sum_send, sum_recv, loc_send, loc_recv, res_send, res_recv, res_pass, res_got,
    gx_send, gx_recv, gy_send, gy_recv, cy_send, cy_recv, cx_send, cx_recv, ro_send, ro_recv, all_send, all_recv, all_pass, all_got, norm_send, norm_recv,
):
    me = lax.axis_index("feat")
    group = lax.axis_index("frames")
    z, q = me // 4, me % 4
    xh, y = group // 4, group % 4
    core = q % 2
    q_sib = q + 1 - 2 * core
    q_x = (q + 2) % 4

    def feat_dev(d, qq):
        return {"feat": ((z + d + 8) % 8) * 4 + qq}

    def frame_dev(k):
        dx, dy = k // 4, k % 4
        return ((xh + dx) % 2) * 4 + (y + dy) % 4

    sibling, neighbour, across = feat_dev(0, q_sib), feat_dev(0, q_x), feat_dev(0, 3 - q)
    sends = []

    def send(src, dst, ssem, rsem, dev):
        copy = pltpu.make_async_remote_copy(
            src_ref=src, dst_ref=dst, send_sem=ssem, recv_sem=rsem, device_id=dev, device_id_type=MESH
        )
        copy.start()
        sends.append(copy)

    def arrived(ref, rsem):
        pltpu.make_async_remote_copy(
            src_ref=ref, dst_ref=ref, send_sem=x_send.at[0], recv_sem=rsem, device_id=sibling, device_id_type=MESH
        ).wait_recv()

    local = [
        pltpu.make_async_copy(src, dst, local_sem.at[i])
        for i, (src, dst) in enumerate(
            ((x_hbm, x_all.at[0, q]), (shift_hbm, shift), (proj_hbm, proj), (w_hbm, w), (labels_hbm, labels), (readout_hbm, readout))
        )
    ]
    for copy in local:
        copy.start()

    barrier = pltpu.get_barrier_semaphore()
    partners = [feat_dev(d, q) for d in OFFS[1:]] + [neighbour, across, sibling]
    partners += [{"frames": frame_dev(k)} for k in range(1, 8)]
    for dev in partners:
        pl.semaphore_signal(barrier, inc=1, device_id=dev, device_id_type=MESH)
    pl.semaphore_wait(barrier, len(partners))

    def gather_local(s):
        piece = x_all.at[s, q]
        source = piece if s else x_hbm
        if s:
            arrived(piece, x_recv.at[s, 0])
        send(source, piece, x_send.at[8 + s], x_recv.at[s, 2], neighbour)
        send(source, piece, x_send.at[24 + s], x_recv.at[s, 3], across)
        send(source, piece, x_send.at[16 + s], x_recv.at[s, 1], sibling)

    def gather_wait(s):
        arrived(x_all.at[s, q_sib], x_recv.at[s, 1])
        arrived(x_all.at[s, q_x], x_recv.at[s, 2])
        arrived(x_all.at[s, 3 - q], x_recv.at[s, 3])

    def x_local(*slots):
        for s in slots:
            gather_local(s)

    def x_wait(*slots):
        for s in slots:
            gather_wait(s)

    gather_local(0)
    for s in range(1, 8):
        m = MIRROR[s]
        send(x_hbm, x_all.at[m, q], x_send.at[s], x_recv.at[m, 0], feat_dev(OFFS[s], q))

    w_low[144:ROWS, :] = jnp.zeros((ROWS - 144, w_low.shape[1]), BF16)
    local[3].wait()
    w_low[0:classes, :] = w[...].astype(BF16)
    local[1].wait()
    local[2].wait()
    local[0].wait()

    nt = (((1,), (1,)), ((), ()))
    turn = 1.0 / (2.0 * math.pi)
    scale = scale_ref[0] * turn

    def half(chunk, first):
        lo, hi = CHUNKS[chunk]
        n = (hi - lo) * 128
        xs = x_all[lo:hi].reshape(n, x_all.shape[-1])

        def block(j, carry):
            cols = pl.ds(pl.multiple_of(j * NB, NB), NB)
            product = jnp.dot(xs, proj[:, cols], preferred_element_type=F32)
            feats[lo * 128 : hi * 128, cols] = features_of(product, scale, shift[:, cols] * turn)
            return carry

        count = feats.shape[1] // NB // 2
        lax.fori_loop(first * count, (first + 1) * count, block, 0, unroll=True)

    def scores(chunk):
        lo, hi = CHUNKS[chunk]
        part = lax.dot_general(w_low[...], feats[lo * 128 : hi * 128, :], nt, preferred_element_type=F32)
        for s in range(lo, hi):
            kept[s] = part[:, (s - lo) * 128 : (s - lo + 1) * 128].reshape(2, ROWS // 2, 128)
            pair_out[s] = kept[s, 1 - core].astype(BF16)
            send(pair_out.at[s], pair_in.at[s], pair_send.at[s], pair_recv.at[s], sibling)

    def pass_on(chunk):
        for s in range(*CHUNKS[chunk]):
            arrived(pair_in.at[s], pair_recv.at[s])
            both = kept[s, core] + pair_in[s].astype(F32)
            if s == 0:
                return both
            m = MIRROR[s]
            sum_out[s] = both.astype(BF16)
            send(sum_out.at[s], sum_in.at[m], sum_send.at[s], sum_recv.at[m], feat_dev(OFFS[s], q))

    x_local(1, 2)
    x_wait(0)
    half(0, 0)
    x_local(3, 4)
    half(0, 1)
    scores(0)
    x_local(5, 6)
    x_wait(1, 2)
    half(1, 0)
    total = pass_on(0)
    x_local(7)
    half(1, 1)
    scores(1)
    x_wait(3, 4)
    half(2, 0)
    pass_on(1)
    half(2, 1)
    scores(2)
    x_wait(5, 6)
    half(3, 0)
    pass_on(2)
    half(3, 1)
    scores(3)
    x_wait(7)
    half(4, 0)
    pass_on(3)
    half(4, 1)
    scores(4)

    local[4].wait()
    local[5].wait()
    ro = readout[...]
    ro_hi = ro.astype(BF16)
    rest = ro - ro_hi.astype(F32)
    ro_mid = rest.astype(BF16)
    ro_lo = (rest - ro_mid.astype(F32)).astype(BF16)
    x0 = x_all[0].reshape(128, x_all.shape[-1])
    linear = (
        lax.dot_general(ro_hi, x0, nt, preferred_element_type=F32)
        + lax.dot_general(ro_mid, x0, nt, preferred_element_type=F32)
        + lax.dot_general(ro_lo, x0, nt, preferred_element_type=F32)
    )
    linear = jnp.concatenate([linear, jnp.zeros((ROWS - classes, 128), F32)], axis=0)
    pass_on(4)

    for s in range(1, 8):
        arrived(sum_in.at[s], sum_recv.at[s])
        total = total + sum_in[s].astype(F32)
    loc[0] = total.astype(BF16)
    send(loc.at[0], loc.at[2], loc_send.at[0], loc_recv.at[2], neighbour)
    send(loc.at[0], loc.at[3], loc_send.at[1], loc_recv.at[3], across)
    send(loc.at[0], loc.at[1], loc_send.at[2], loc_recv.at[1], sibling)
    for k in range(1, 4):
        arrived(loc.at[k], loc_recv.at[k])
    final[core] = loc[0].astype(F32) + loc[2].astype(F32)
    final[1 - core] = loc[1].astype(F32) + loc[3].astype(F32)
    total = final[...].reshape(ROWS, 128)
    rows = lax.broadcasted_iota(jnp.int32, (ROWS, 128), 0)
    inside = rows < classes
    value = jnp.where(inside, total * (1.0 / math.sqrt(feat_total)) + linear, -1e30)
    value = jnp.exp(value - jnp.max(value, axis=0, keepdims=True))
    probs = value / jnp.sum(value, axis=0, keepdims=True)
    label = labels[pl.ds(z, 1), :]
    residual = jnp.where(rows == label, probs - 1.0, probs)
    res_all[0] = residual.astype(BF16).reshape(2, ROWS // 2, 128)

    for s in range(1, 8):
        m = MIRROR[s]
        send(res_all.at[0, core], res_all.at[m, core], res_send.at[s], res_recv.at[m], feat_dev(OFFS[s], q))
    for s in range(1, 8):
        piece = res_all.at[s, core]
        arrived(piece, res_recv.at[s])
        send(piece, piece, res_pass.at[s], res_got.at[s], sibling)
    for s in range(8):
        if s:
            arrived(res_all.at[s, 1 - core], res_got.at[s])
        res_t[:, s * 128 : (s + 1) * 128] = res_all[s].reshape(ROWS, 128)

    cols_each = out_ref.shape[1]

    def grad_block(k):
        cols = pl.ds(pl.multiple_of(frame_dev(k) * cols_each, cols_each), cols_each)
        return jnp.dot(res_t[...], feats[:, cols], preferred_element_type=F32)

    back = [0] + [(k // 4) * 4 + (4 - k % 4) % 4 for k in range(1, 8)]
    opposite = {"frames": frame_dev(4)}

    def grad_send_blocks(dy):
        far, near = grad_block(4 + dy), grad_block(dy)
        gx_out[dy] = far[:, :XF].astype(BF16)
        send(gx_out.at[dy], gx_in.at[dy], gx_send.at[dy], gx_recv.at[dy], opposite)
        kx[dy] = near[:, :XF]
        if dy:
            gy_out[dy, 0] = near[:, XF:].astype(BF16)
            gy_out[dy, 1] = far[:, XF:].astype(BF16)
            send(gy_out.at[dy], gy_in.at[4 - dy], gy_send.at[dy], gy_recv.at[4 - dy], {"frames": frame_dev(dy)})
        else:
            ky[0] = near[:, XF:]
            ky[1] = far[:, XF:]

    grad_send_blocks(2)

    ro_pad[...] = jnp.zeros_like(ro_pad)
    depth = x_all.shape[-1]
    ro_pad[0:ROWS, 0:depth] = jnp.dot(res_t[...], x_all[...].reshape(1024, depth), preferred_element_type=F32)
    ro_mine = ro_pad[pl.ds(pl.multiple_of(z * 32, 32), 32), pl.ds(pl.multiple_of(core * 256, 256), 256)]
    ro_out[...] = ro_mine.astype(BF16)
    for k in range(1, 8):
        b = back[k]
        send(ro_out, ro_in.at[b], ro_send.at[k], ro_recv.at[b], {"frames": frame_dev(k)})

    for dy in (1, 3, 0):
        grad_send_blocks(dy)

    def along_y(dy):
        arrived(gx_in.at[dy], gx_recv.at[dy])
        cy_out[dy] = (kx[dy] + gx_in[dy].astype(F32)).astype(BF16)
        send(cy_out.at[dy], cy_in.at[4 - dy], cy_send.at[dy], cy_recv.at[4 - dy], {"frames": frame_dev(dy)})

    along_y(2)
    rest_own, rest_far = ky[0], ky[1]
    for dy in (1, 3, 2):
        arrived(gy_in.at[dy], gy_recv.at[dy])
        rest_own = rest_own + gy_in[dy, 0].astype(F32)
        rest_far = rest_far + gy_in[dy, 1].astype(F32)
    cx[0] = rest_far.astype(BF16)
    send(cx.at[0], cx.at[1], cx_send.at[0], cx_recv.at[0], opposite)
    along_y(1)
    for k in range(1, 8):
        arrived(ro_in.at[k], ro_recv.at[k])
        ro_mine = ro_mine + ro_in[k].astype(F32)
    ro_all[z, core] = ro_mine.astype(BF16)
    mine = ro_all.at[z, core]
    for s in range(1, 8):
        send(mine, mine, all_send.at[s], all_recv.at[MIRROR[s]], feat_dev(OFFS[s], q))
    send(mine, mine, all_pass.at[0], all_got.at[0], sibling)
    along_y(3)

    arrived(gx_in.at[0], gx_recv.at[0])
    own_grad = kx[0] + gx_in[0].astype(F32)
    arrived(cx.at[1], cx_recv.at[0])
    rest_own = rest_own + cx[1].astype(F32)
    for dy in (2, 1, 3):
        arrived(cy_in.at[dy], cy_recv.at[dy])
        own_grad = own_grad + cy_in[dy].astype(F32)
    own_grad = jnp.concatenate([own_grad, rest_own], axis=1)
    cols = pl.ds(pl.multiple_of(group * cols_each, cols_each), cols_each)
    stepped = w[:, cols] - (5.0 / math.sqrt(batch)) * own_grad[:classes]
    trimmed = stepped - jnp.clip(stepped, -1.0, 1.0)
    part = jnp.sum(trimmed * trimmed, axis=0, keepdims=True)
    part = part[:, 0:128] + part[:, 128:256] + part[:, 256:384] + part[:, 384:512]
    norm_out[...] = jnp.broadcast_to(part, (8, 128))
    for k in range(1, 8):
        b = back[k]
        send(norm_out, norm_in.at[b], norm_send.at[k], norm_recv.at[b], {"frames": frame_dev(k)})
    for s in range(1, 8):
        piece = ro_all.at[(z + OFFS[s] + 8) % 8, core]
        arrived(piece, all_recv.at[s])
        send(piece, piece, all_pass.at[s], all_got.at[s], sibling)
    for s in range(8):
        arrived(ro_all.at[(z + OFFS[s] + 8) % 8, 1 - core], all_got.at[s])
    for i in range(0, classes, 32):
        n = min(32, classes - i)
        grad = jnp.concatenate([ro_all[i // 32, k] for k in range(2)], axis=1).astype(F32)
        readout_out_ref[i : i + n, :] = ro[i : i + n] - (3.0 / math.sqrt(batch)) * grad[:n, :depth]
    for k in range(1, 8):
        arrived(norm_in.at[k], norm_recv.at[k])
        part = part + norm_in[k, 0:1, :]
    norm = jnp.sqrt(jnp.sum(part, axis=1, keepdims=True) + 1e-6)
    limit = 1.5 * math.sqrt(w.shape[0] * w.shape[1])
    out_ref[...] = trimmed * jnp.maximum(0.0, 1.0 - limit / norm)

    for copy in sends:
        copy.wait_send()


def body(frames_in, labels, projection, kernel_scale, shift, weights, readout):
    n_feat, n_frames = lax.axis_size("feat"), lax.axis_size("frames")
    rows, depth = frames_in.shape
    classes, columns = weights.shape
    batch = labels.shape[0] * n_frames
    each = columns // n_frames
    vmem = pl.BlockSpec(memory_space=pltpu.VMEM)
    hbm = pl.BlockSpec(memory_space=pl.ANY)
    dma = pltpu.SemaphoreType.DMA
    return pl.pallas_call(
        functools.partial(kernel, batch, columns * n_feat, classes),
        out_shape=(
            pltpu.VMEM((classes, each), F32),
            pltpu.VMEM(readout.shape, F32),
        ),
        in_specs=[pl.BlockSpec(memory_space=pltpu.SMEM)] + [hbm] * 6,
        out_specs=(vmem, vmem),
        scratch_shapes=[
            pltpu.VMEM((depth, columns), BF16),
            pltpu.VMEM((classes, columns), F32),
            pltpu.VMEM((8, 128), jnp.int32),
            pltpu.VMEM((1, columns), F32),
            pltpu.VMEM(readout.shape, F32),
            pltpu.VMEM((ROWS, columns), BF16),
            pltpu.VMEM((8, 4, rows, depth), BF16),
            pltpu.VMEM((1024, columns), BF16),
            pltpu.VMEM((8, 2, ROWS // 2, 128), F32),
            pltpu.VMEM((8, ROWS // 2, 128), BF16),
            pltpu.VMEM((8, ROWS // 2, 128), BF16),
            pltpu.VMEM((8, ROWS // 2, 128), BF16),
            pltpu.VMEM((8, ROWS // 2, 128), BF16),
            pltpu.VMEM((4, ROWS // 2, 128), BF16),
            pltpu.VMEM((2, ROWS // 2, 128), F32),
            pltpu.VMEM((8, 2, ROWS // 2, 128), BF16),
            pltpu.VMEM((ROWS, 1024), BF16),
            pltpu.VMEM((4, ROWS, XF), BF16),
            pltpu.VMEM((4, ROWS, XF), BF16),
            pltpu.VMEM((4, 2, ROWS, each - XF), BF16),
            pltpu.VMEM((4, 2, ROWS, each - XF), BF16),
            pltpu.VMEM((4, ROWS, XF), BF16),
            pltpu.VMEM((4, ROWS, XF), BF16),
            pltpu.VMEM((2, ROWS, each - XF), BF16),
            pltpu.VMEM((4, ROWS, XF), F32),
            pltpu.VMEM((2, ROWS, each - XF), F32),
            pltpu.VMEM((256, 512), F32),
            pltpu.VMEM((32, 256), BF16),
            pltpu.VMEM((8, 32, 256), BF16),
            pltpu.VMEM((8, 2, 32, 256), BF16),
            pltpu.VMEM((8, 128), F32),
            pltpu.VMEM((8, 8, 128), F32),
            dma((6,)),
            dma((32,)), dma((8, 4)),
            dma((8,)), dma((8,)),
            dma((8,)), dma((8,)),
            dma((3,)), dma((4,)),
            dma((8,)), dma((8,)), dma((8,)), dma((8,)),
            dma((4,)), dma((4,)),
            dma((4,)), dma((4,)),
            dma((4,)), dma((4,)),
            dma((1,)), dma((1,)),
            dma((8,)), dma((8,)),
            dma((8,)), dma((8,)), dma((8,)), dma((8,)),
            dma((8,)), dma((8,)),
        ],
        compiler_params=pltpu.CompilerParams(
            collective_id=0, has_side_effects=True, vmem_limit_bytes=56 * 2**20
        ),
        name="fourier_step",
    )(kernel_scale, frames_in, projection, weights, labels.reshape(8, 128), shift.reshape(1, -1), readout)


def solution(mesh):
    return jax.shard_map(
        body,
        mesh=mesh,
        in_specs=(
            P(("frames", "feat"), None),
            P("frames"),
            P(None, "feat"),
            P("feat"),
            P("feat"),
            P(None, "feat"),
            P(),
        ),
        out_specs=(P(None, ("feat", "frames")), P()),
        check_vma=False,
    )
```

```python
import functools
import math

import jax
import jax.numpy as jnp
from jax import lax
from jax.experimental import pallas as pl
from jax.experimental.pallas import tpu as pltpu
from jax.sharding import PartitionSpec as P

MESH = pl.DeviceIdType.MESH
F32, BF16 = jnp.float32, jnp.bfloat16
ROWS = 160
NB = 256
XF = 256

OFFS = (0, 1, -1, 2, -2, 3, -3, 4)
MIRROR = tuple(OFFS.index(-d) if -d in OFFS else OFFS.index(d) for d in OFFS)
CHUNKS = ((0, 1), (1, 3), (3, 5), (5, 7), (7, 8))

COS = (1.4142124652862549, -27.91513442993164, 91.82299041748047, -120.59228515625, 83.1423110961914, -29.799043655395508)


def features_of(product, scale, shift):
    turns = product * scale + shift
    r = turns - jnp.round(turns)
    u = r * r
    acc = COS[-1] * u + COS[-2]
    for c in COS[-3::-1]:
        acc = acc * u + c
    return acc.astype(BF16)


def kernel(
    batch, feat_total, classes,
    scale_ref, x_hbm, proj_hbm, w_hbm, labels_hbm, shift_hbm, readout_hbm,
    out_ref, readout_out_ref,
    proj, w, labels, shift, readout, w_low, x_all, feats, kept, pair_out, pair_in, sum_out, sum_in, loc, final, res_all, res_t,
    gx_out, gx_in, gy_out, gy_in, cy_out, cy_in, cx, kx, ky, ro_pad, ro_out, ro_in, ro_all, norm_out, norm_in,
    local_sem, far_z, far_x, x_send, x_recv, pair_send, pair_recv, sum_send, sum_recv, loc_send, loc_recv, res_send, res_recv, res_pass, res_got,
    gx_send, gx_recv, gy_send, gy_recv, cy_send, cy_recv, cx_send, cx_recv, ro_send, ro_recv, all_send, all_recv, all_pass, all_got, norm_send, norm_recv,
):
    me = lax.axis_index("feat")
    group = lax.axis_index("frames")
    z, q = me // 4, me % 4
    xh, y = group // 4, group % 4
    core = q % 2
    q_sib = q + 1 - 2 * core
    q_x = (q + 2) % 4

    def feat_dev(d, qq):
        return {"feat": ((z + d + 8) % 8) * 4 + qq}

    def frame_dev(k):
        dx, dy = k // 4, k % 4
        return ((xh + dx) % 2) * 4 + (y + dy) % 4

    sibling, neighbour, across = feat_dev(0, q_sib), feat_dev(0, q_x), feat_dev(0, 3 - q)
    sends = []

    def send(src, dst, ssem, rsem, dev):
        copy = pltpu.make_async_remote_copy(
            src_ref=src, dst_ref=dst, send_sem=ssem, recv_sem=rsem, device_id=dev, device_id_type=MESH
        )
        copy.start()
        sends.append(copy)

    def arrived(ref, rsem):
        pltpu.make_async_remote_copy(
            src_ref=ref, dst_ref=ref, send_sem=x_send.at[0], recv_sem=rsem, device_id=sibling, device_id_type=MESH
        ).wait_recv()

    local = [
        pltpu.make_async_copy(src, dst, local_sem.at[i])
        for i, (src, dst) in enumerate(
            ((x_hbm, x_all.at[0, q]), (shift_hbm, shift), (proj_hbm, proj), (w_hbm, w), (labels_hbm, labels), (readout_hbm, readout))
        )
    ]
    for copy in local:
        copy.start()

    barrier = pltpu.get_barrier_semaphore()
    partners = [feat_dev(d, q) for d in OFFS[1:5]] + [neighbour, across, sibling]
    partners += [{"frames": frame_dev(k)} for k in range(1, 5)]
    for dev in partners:
        pl.semaphore_signal(barrier, inc=1, device_id=dev, device_id_type=MESH)
    pl.semaphore_wait(barrier, len(partners))
    for d in (2, -2):
        pl.semaphore_signal(far_z, inc=1, device_id=feat_dev(d, q), device_id_type=MESH)
    pl.semaphore_signal(far_x, inc=1, device_id={"frames": frame_dev(4)}, device_id_type=MESH)

    def gather_local(s):
        piece = x_all.at[s, q]
        source = piece if s else x_hbm
        if s:
            arrived(piece, x_recv.at[s, 0])
        send(source, piece, x_send.at[8 + s], x_recv.at[s, 2], neighbour)
        send(source, piece, x_send.at[24 + s], x_recv.at[s, 3], across)
        send(source, piece, x_send.at[16 + s], x_recv.at[s, 1], sibling)

    def gather_wait(s):
        arrived(x_all.at[s, q_sib], x_recv.at[s, 1])
        arrived(x_all.at[s, q_x], x_recv.at[s, 2])
        arrived(x_all.at[s, 3 - q], x_recv.at[s, 3])

    def x_local(*slots):
        for s in slots:
            gather_local(s)

    def x_wait(*slots):
        for s in slots:
            gather_wait(s)

    gather_local(0)

    def gather_z(slots):
        for s in slots:
            m = MIRROR[s]
            send(x_hbm, x_all.at[m, q], x_send.at[s], x_recv.at[m, 0], feat_dev(OFFS[s], q))

    gather_z((1, 2, 3, 4))

    w_low[144:ROWS, :] = jnp.zeros((ROWS - 144, w_low.shape[1]), BF16)
    local[3].wait()
    w_low[0:classes, :] = w[...].astype(BF16)
    pl.semaphore_wait(far_z, 2)
    gather_z((5, 6, 7))
    local[1].wait()
    local[2].wait()
    local[0].wait()

    nt = (((1,), (1,)), ((), ()))
    turn = 1.0 / (2.0 * math.pi)
    scale = scale_ref[0] * turn

    def half(chunk, first):
        lo, hi = CHUNKS[chunk]
        n = (hi - lo) * 128
        xs = x_all[lo:hi].reshape(n, x_all.shape[-1])

        def block(j, carry):
            cols = pl.ds(pl.multiple_of(j * NB, NB), NB)
            product = jnp.dot(xs, proj[:, cols], preferred_element_type=F32)
            feats[lo * 128 : hi * 128, cols] = features_of(product, scale, shift[:, cols] * turn)
            return carry

        count = feats.shape[1] // NB // 2
        lax.fori_loop(first * count, (first + 1) * count, block, 0, unroll=True)

    def scores(chunk):
        lo, hi = CHUNKS[chunk]
        part = lax.dot_general(w_low[...], feats[lo * 128 : hi * 128, :], nt, preferred_element_type=F32)
        for s in range(lo, hi):
            kept[s] = part[:, (s - lo) * 128 : (s - lo + 1) * 128].reshape(2, ROWS // 2, 128)
            pair_out[s] = kept[s, 1 - core].astype(BF16)
            send(pair_out.at[s], pair_in.at[s], pair_send.at[s], pair_recv.at[s], sibling)

    def pass_on(chunk):
        for s in range(*CHUNKS[chunk]):
            arrived(pair_in.at[s], pair_recv.at[s])
            both = kept[s, core] + pair_in[s].astype(F32)
            if s == 0:
                return both
            m = MIRROR[s]
            sum_out[s] = both.astype(BF16)
            send(sum_out.at[s], sum_in.at[m], sum_send.at[s], sum_recv.at[m], feat_dev(OFFS[s], q))

    x_local(1, 2)
    x_wait(0)
    half(0, 0)
    x_local(3, 4)
    half(0, 1)
    scores(0)
    x_local(5, 6)
    x_wait(1, 2)
    half(1, 0)
    total = pass_on(0)
    x_local(7)
    half(1, 1)
    scores(1)
    x_wait(3, 4)
    half(2, 0)
    pass_on(1)
    half(2, 1)
    scores(2)
    x_wait(5, 6)
    half(3, 0)
    pass_on(2)
    half(3, 1)
    scores(3)
    x_wait(7)
    half(4, 0)
    pass_on(3)
    half(4, 1)
    scores(4)

    local[4].wait()
    local[5].wait()
    ro = readout[...]
    ro_hi = ro.astype(BF16)
    rest = ro - ro_hi.astype(F32)
    ro_mid = rest.astype(BF16)
    ro_lo = (rest - ro_mid.astype(F32)).astype(BF16)
    x0 = x_all[0].reshape(128, x_all.shape[-1])
    linear = (
        lax.dot_general(ro_hi, x0, nt, preferred_element_type=F32)
        + lax.dot_general(ro_mid, x0, nt, preferred_element_type=F32)
        + lax.dot_general(ro_lo, x0, nt, preferred_element_type=F32)
    )
    linear = jnp.concatenate([linear, jnp.zeros((ROWS - classes, 128), F32)], axis=0)
    pass_on(4)

    for s in range(1, 8):
        arrived(sum_in.at[s], sum_recv.at[s])
        total = total + sum_in[s].astype(F32)
    loc[0] = total.astype(BF16)
    send(loc.at[0], loc.at[2], loc_send.at[0], loc_recv.at[2], neighbour)
    send(loc.at[0], loc.at[3], loc_send.at[1], loc_recv.at[3], across)
    send(loc.at[0], loc.at[1], loc_send.at[2], loc_recv.at[1], sibling)
    for k in range(1, 4):
        arrived(loc.at[k], loc_recv.at[k])
    final[core] = loc[0].astype(F32) + loc[2].astype(F32)
    final[1 - core] = loc[1].astype(F32) + loc[3].astype(F32)
    total = final[...].reshape(ROWS, 128)
    rows = lax.broadcasted_iota(jnp.int32, (ROWS, 128), 0)
    inside = rows < classes
    value = jnp.where(inside, total * (1.0 / math.sqrt(feat_total)) + linear, -1e30)
    value = jnp.exp(value - jnp.max(value, axis=0, keepdims=True))
    probs = value / jnp.sum(value, axis=0, keepdims=True)
    label = labels[pl.ds(z, 1), :]
    residual = jnp.where(rows == label, probs - 1.0, probs)
    res_all[0] = residual.astype(BF16).reshape(2, ROWS // 2, 128)

    for s in range(1, 8):
        m = MIRROR[s]
        send(res_all.at[0, core], res_all.at[m, core], res_send.at[s], res_recv.at[m], feat_dev(OFFS[s], q))
    for s in range(1, 8):
        piece = res_all.at[s, core]
        arrived(piece, res_recv.at[s])
        send(piece, piece, res_pass.at[s], res_got.at[s], sibling)
    for s in range(8):
        if s:
            arrived(res_all.at[s, 1 - core], res_got.at[s])
        res_t[:, s * 128 : (s + 1) * 128] = res_all[s].reshape(ROWS, 128)

    cols_each = out_ref.shape[1]

    def grad_block(k):
        cols = pl.ds(pl.multiple_of(frame_dev(k) * cols_each, cols_each), cols_each)
        return jnp.dot(res_t[...], feats[:, cols], preferred_element_type=F32)

    back = [0] + [(k // 4) * 4 + (4 - k % 4) % 4 for k in range(1, 8)]
    opposite = {"frames": frame_dev(4)}

    def grad_send_blocks(dy):
        far, near = grad_block(4 + dy), grad_block(dy)
        gx_out[dy] = far[:, :XF].astype(BF16)
        send(gx_out.at[dy], gx_in.at[dy], gx_send.at[dy], gx_recv.at[dy], opposite)
        kx[dy] = near[:, :XF]
        if dy:
            gy_out[dy, 0] = near[:, XF:].astype(BF16)
            gy_out[dy, 1] = far[:, XF:].astype(BF16)
            send(gy_out.at[dy], gy_in.at[4 - dy], gy_send.at[dy], gy_recv.at[4 - dy], {"frames": frame_dev(dy)})
        else:
            ky[0] = near[:, XF:]
            ky[1] = far[:, XF:]

    grad_send_blocks(2)

    pl.semaphore_wait(far_x, 1)
    ro_pad[...] = jnp.zeros_like(ro_pad)
    depth = x_all.shape[-1]
    ro_pad[0:ROWS, 0:depth] = jnp.dot(res_t[...], x_all[...].reshape(1024, depth), preferred_element_type=F32)
    ro_mine = ro_pad[pl.ds(pl.multiple_of(z * 32, 32), 32), pl.ds(pl.multiple_of(core * 256, 256), 256)]
    ro_out[...] = ro_mine.astype(BF16)
    for k in range(1, 8):
        b = back[k]
        send(ro_out, ro_in.at[b], ro_send.at[k], ro_recv.at[b], {"frames": frame_dev(k)})

    for dy in (1, 3, 0):
        grad_send_blocks(dy)

    def along_y(dy):
        arrived(gx_in.at[dy], gx_recv.at[dy])
        cy_out[dy] = (kx[dy] + gx_in[dy].astype(F32)).astype(BF16)
        send(cy_out.at[dy], cy_in.at[4 - dy], cy_send.at[dy], cy_recv.at[4 - dy], {"frames": frame_dev(dy)})

    along_y(2)
    rest_own, rest_far = ky[0], ky[1]
    for dy in (1, 3, 2):
        arrived(gy_in.at[dy], gy_recv.at[dy])
        rest_own = rest_own + gy_in[dy, 0].astype(F32)
        rest_far = rest_far + gy_in[dy, 1].astype(F32)
    cx[0] = rest_far.astype(BF16)
    send(cx.at[0], cx.at[1], cx_send.at[0], cx_recv.at[0], opposite)
    along_y(1)
    for k in range(1, 8):
        arrived(ro_in.at[k], ro_recv.at[k])
        ro_mine = ro_mine + ro_in[k].astype(F32)
    ro_all[z, core] = ro_mine.astype(BF16)
    mine = ro_all.at[z, core]
    for s in range(1, 8):
        send(mine, mine, all_send.at[s], all_recv.at[MIRROR[s]], feat_dev(OFFS[s], q))
    send(mine, mine, all_pass.at[0], all_got.at[0], sibling)
    along_y(3)

    arrived(gx_in.at[0], gx_recv.at[0])
    own_grad = kx[0] + gx_in[0].astype(F32)
    arrived(cx.at[1], cx_recv.at[0])
    rest_own = rest_own + cx[1].astype(F32)
    for dy in (2, 1, 3):
        arrived(cy_in.at[dy], cy_recv.at[dy])
        own_grad = own_grad + cy_in[dy].astype(F32)
    own_grad = jnp.concatenate([own_grad, rest_own], axis=1)
    cols = pl.ds(pl.multiple_of(group * cols_each, cols_each), cols_each)
    stepped = w[:, cols] - (5.0 / math.sqrt(batch)) * own_grad[:classes]
    trimmed = stepped - jnp.clip(stepped, -1.0, 1.0)
    part = jnp.sum(trimmed * trimmed, axis=0, keepdims=True)
    part = part[:, 0:128] + part[:, 128:256] + part[:, 256:384] + part[:, 384:512]
    norm_out[...] = jnp.broadcast_to(part, (8, 128))
    for k in range(1, 8):
        b = back[k]
        send(norm_out, norm_in.at[b], norm_send.at[k], norm_recv.at[b], {"frames": frame_dev(k)})
    for s in range(1, 8):
        piece = ro_all.at[(z + OFFS[s] + 8) % 8, core]
        arrived(piece, all_recv.at[s])
        send(piece, piece, all_pass.at[s], all_got.at[s], sibling)
    for s in range(8):
        arrived(ro_all.at[(z + OFFS[s] + 8) % 8, 1 - core], all_got.at[s])
    for i in range(0, classes, 32):
        n = min(32, classes - i)
        grad = jnp.concatenate([ro_all[i // 32, k] for k in range(2)], axis=1).astype(F32)
        readout_out_ref[i : i + n, :] = ro[i : i + n] - (3.0 / math.sqrt(batch)) * grad[:n, :depth]
    for k in range(1, 8):
        arrived(norm_in.at[k], norm_recv.at[k])
        part = part + norm_in[k, 0:1, :]
    norm = jnp.sqrt(jnp.sum(part, axis=1, keepdims=True) + 1e-6)
    limit = 1.5 * math.sqrt(w.shape[0] * w.shape[1])
    out_ref[...] = trimmed * jnp.maximum(0.0, 1.0 - limit / norm)

    for copy in sends:
        copy.wait_send()


def body(frames_in, labels, projection, kernel_scale, shift, weights, readout):
    n_feat, n_frames = lax.axis_size("feat"), lax.axis_size("frames")
    rows, depth = frames_in.shape
    classes, columns = weights.shape
    batch = labels.shape[0] * n_frames
    each = columns // n_frames
    vmem = pl.BlockSpec(memory_space=pltpu.VMEM)
    hbm = pl.BlockSpec(memory_space=pl.ANY)
    dma = pltpu.SemaphoreType.DMA
    return pl.pallas_call(
        functools.partial(kernel, batch, columns * n_feat, classes),
        out_shape=(
            pltpu.VMEM((classes, each), F32),
            pltpu.VMEM(readout.shape, F32),
        ),
        in_specs=[pl.BlockSpec(memory_space=pltpu.SMEM)] + [hbm] * 6,
        out_specs=(vmem, vmem),
        scratch_shapes=[
            pltpu.VMEM((depth, columns), BF16),
            pltpu.VMEM((classes, columns), F32),
            pltpu.VMEM((8, 128), jnp.int32),
            pltpu.VMEM((1, columns), F32),
            pltpu.VMEM(readout.shape, F32),
            pltpu.VMEM((ROWS, columns), BF16),
            pltpu.VMEM((8, 4, rows, depth), BF16),
            pltpu.VMEM((1024, columns), BF16),
            pltpu.VMEM((8, 2, ROWS // 2, 128), F32),
            pltpu.VMEM((8, ROWS // 2, 128), BF16),
            pltpu.VMEM((8, ROWS // 2, 128), BF16),
            pltpu.VMEM((8, ROWS // 2, 128), BF16),
            pltpu.VMEM((8, ROWS // 2, 128), BF16),
            pltpu.VMEM((4, ROWS // 2, 128), BF16),
            pltpu.VMEM((2, ROWS // 2, 128), F32),
            pltpu.VMEM((8, 2, ROWS // 2, 128), BF16),
            pltpu.VMEM((ROWS, 1024), BF16),
            pltpu.VMEM((4, ROWS, XF), BF16),
            pltpu.VMEM((4, ROWS, XF), BF16),
            pltpu.VMEM((4, 2, ROWS, each - XF), BF16),
            pltpu.VMEM((4, 2, ROWS, each - XF), BF16),
            pltpu.VMEM((4, ROWS, XF), BF16),
            pltpu.VMEM((4, ROWS, XF), BF16),
            pltpu.VMEM((2, ROWS, each - XF), BF16),
            pltpu.VMEM((4, ROWS, XF), F32),
            pltpu.VMEM((2, ROWS, each - XF), F32),
            pltpu.VMEM((256, 512), F32),
            pltpu.VMEM((32, 256), BF16),
            pltpu.VMEM((8, 32, 256), BF16),
            pltpu.VMEM((8, 2, 32, 256), BF16),
            pltpu.VMEM((8, 128), F32),
            pltpu.VMEM((8, 8, 128), F32),
            dma((6,)),
            pltpu.SemaphoreType.REGULAR,
            pltpu.SemaphoreType.REGULAR,
            dma((32,)), dma((8, 4)),
            dma((8,)), dma((8,)),
            dma((8,)), dma((8,)),
            dma((3,)), dma((4,)),
            dma((8,)), dma((8,)), dma((8,)), dma((8,)),
            dma((4,)), dma((4,)),
            dma((4,)), dma((4,)),
            dma((4,)), dma((4,)),
            dma((1,)), dma((1,)),
            dma((8,)), dma((8,)),
            dma((8,)), dma((8,)), dma((8,)), dma((8,)),
            dma((8,)), dma((8,)),
        ],
        compiler_params=pltpu.CompilerParams(
            collective_id=0, has_side_effects=True, vmem_limit_bytes=56 * 2**20
        ),
        name="fourier_step",
    )(kernel_scale, frames_in, projection, weights, labels.reshape(8, 128), shift.reshape(1, -1), readout)


def solution(mesh):
    return jax.shard_map(
        body,
        mesh=mesh,
        in_specs=(
            P(("frames", "feat"), None),
            P("frames"),
            P(None, "feat"),
            P("feat"),
            P("feat"),
            P(None, "feat"),
            P(),
        ),
        out_specs=(P(None, ("feat", "frames")), P()),
        check_vma=False,
    )
```

```python
import functools
import math

import jax
import jax.numpy as jnp
from jax import lax
from jax.experimental import pallas as pl
from jax.experimental.pallas import tpu as pltpu
from jax.sharding import PartitionSpec as P

MESH = pl.DeviceIdType.MESH
F32, BF16 = jnp.float32, jnp.bfloat16
ROWS = 160
NB = 256
XF = 256

OFFS = (0, 1, -1, 2, -2, 3, -3, 4)
MIRROR = tuple(OFFS.index(-d) if -d in OFFS else OFFS.index(d) for d in OFFS)
CHUNKS = ((0, 1), (1, 3), (3, 5), (5, 7), (7, 8))

COS = (1.4142124652862549, -27.91513442993164, 91.82299041748047, -120.59228515625, 83.1423110961914, -29.799043655395508)


def features_of(product, scale, shift):
    turns = product * scale + shift
    r = turns - jnp.round(turns)
    u = r * r
    acc = COS[-1] * u + COS[-2]
    for c in COS[-3::-1]:
        acc = acc * u + c
    return acc.astype(BF16)


def kernel(
    batch, feat_total, classes,
    scale_ref, x_hbm, proj_hbm, w_hbm, labels_hbm, shift_hbm, readout_hbm,
    out_ref, readout_out_ref,
    proj, w, labels, shift, readout, w_low, x_all, feats, kept, pair_out, pair_in, sum_out, sum_in, loc, final, res_all, res_t,
    gx_out, gx_in, gy_out, gy_in, cy_out, cy_in, cx, kx, ky, ro_pad, ro_out, ro_in, ro_all, norm_out, norm_in,
    local_sem, far_z, far_x, x_send, x_recv, pair_send, pair_recv, sum_send, sum_recv, loc_send, loc_recv, res_send, res_recv, res_pass, res_got,
    gx_send, gx_recv, gy_send, gy_recv, cy_send, cy_recv, cx_send, cx_recv, ro_send, ro_recv, all_send, all_recv, all_pass, all_got, norm_send, norm_recv,
):
    me = lax.axis_index("feat")
    group = lax.axis_index("frames")
    z, q = me // 4, me % 4
    xh, y = group // 4, group % 4
    core = q % 2
    q_sib = q + 1 - 2 * core
    q_x = (q + 2) % 4

    def feat_dev(d, qq):
        return {"feat": ((z + d + 8) % 8) * 4 + qq}

    def frame_dev(k):
        dx, dy = k // 4, k % 4
        return ((xh + dx) % 2) * 4 + (y + dy) % 4

    sibling, neighbour, across = feat_dev(0, q_sib), feat_dev(0, q_x), feat_dev(0, 3 - q)
    sends = []

    def send(src, dst, ssem, rsem, dev):
        copy = pltpu.make_async_remote_copy(
            src_ref=src, dst_ref=dst, send_sem=ssem, recv_sem=rsem, device_id=dev, device_id_type=MESH
        )
        copy.start()
        sends.append(copy)

    def arrived(ref, rsem):
        pltpu.make_async_remote_copy(
            src_ref=ref, dst_ref=ref, send_sem=x_send.at[0], recv_sem=rsem, device_id=sibling, device_id_type=MESH
        ).wait_recv()

    local = [
        pltpu.make_async_copy(src, dst, local_sem.at[i])
        for i, (src, dst) in enumerate(
            ((x_hbm, x_all.at[0, q]), (shift_hbm, shift), (proj_hbm, proj), (w_hbm, w), (labels_hbm, labels), (readout_hbm, readout))
        )
    ]
    for copy in local:
        copy.start()

    barrier = pltpu.get_barrier_semaphore()
    partners = [feat_dev(d, q) for d in OFFS[1:5]] + [neighbour, across, sibling]
    partners += [{"frames": frame_dev(k)} for k in range(1, 5)]
    for dev in partners:
        pl.semaphore_signal(barrier, inc=1, device_id=dev, device_id_type=MESH)
    pl.semaphore_wait(barrier, len(partners))
    for d in (2, -2):
        pl.semaphore_signal(far_z, inc=1, device_id=feat_dev(d, q), device_id_type=MESH)
    pl.semaphore_signal(far_x, inc=1, device_id={"frames": frame_dev(4)}, device_id_type=MESH)

    def half_of(piece, h):
        return piece.at[16 * h : 16 * h + 16]

    def gather_local(s):
        piece = x_all.at[s, q]
        source = piece if s else x_hbm
        if s == 7:
            for h in range(2):
                arrived(half_of(piece, h), x_recv.at[7 - 7 * h, 0])
        elif s:
            arrived(piece, x_recv.at[s, 0])
        if s in (3, 4):
            on = -1 if s == 3 else 1
            send(piece, x_all.at[s + 2, q], x_send.at[s + 2], x_recv.at[s + 2, 0], feat_dev(on, q))
            h = s - 3
            end = half_of(x_all.at[7, q], h)
            send(half_of(piece, h), end, x_send.at[7 * h], x_recv.at[7 - 7 * h, 0], feat_dev(2 * on, q))
        send(source, piece, x_send.at[8 + s], x_recv.at[s, 2], neighbour)
        send(source, piece, x_send.at[24 + s], x_recv.at[s, 3], across)
        send(source, piece, x_send.at[16 + s], x_recv.at[s, 1], sibling)

    def gather_wait(s):
        arrived(x_all.at[s, q_sib], x_recv.at[s, 1])
        arrived(x_all.at[s, q_x], x_recv.at[s, 2])
        arrived(x_all.at[s, 3 - q], x_recv.at[s, 3])

    def x_local(*slots):
        for s in slots:
            gather_local(s)

    def x_wait(*slots):
        for s in slots:
            gather_wait(s)

    gather_local(0)
    for s in (1, 2, 3, 4):
        m = MIRROR[s]
        send(x_hbm, x_all.at[m, q], x_send.at[s], x_recv.at[m, 0], feat_dev(OFFS[s], q))

    w_low[144:ROWS, :] = jnp.zeros((ROWS - 144, w_low.shape[1]), BF16)
    local[3].wait()
    w_low[0:classes, :] = w[...].astype(BF16)
    local[1].wait()
    local[2].wait()
    local[0].wait()

    nt = (((1,), (1,)), ((), ()))
    turn = 1.0 / (2.0 * math.pi)
    scale = scale_ref[0] * turn

    def half(chunk, first):
        lo, hi = CHUNKS[chunk]
        n = (hi - lo) * 128
        xs = x_all[lo:hi].reshape(n, x_all.shape[-1])

        def block(j, carry):
            cols = pl.ds(pl.multiple_of(j * NB, NB), NB)
            product = jnp.dot(xs, proj[:, cols], preferred_element_type=F32)
            feats[lo * 128 : hi * 128, cols] = features_of(product, scale, shift[:, cols] * turn)
            return carry

        count = feats.shape[1] // NB // 2
        lax.fori_loop(first * count, (first + 1) * count, block, 0, unroll=True)

    def scores(chunk):
        lo, hi = CHUNKS[chunk]
        part = lax.dot_general(w_low[...], feats[lo * 128 : hi * 128, :], nt, preferred_element_type=F32)
        for s in range(lo, hi):
            kept[s] = part[:, (s - lo) * 128 : (s - lo + 1) * 128].reshape(2, ROWS // 2, 128)
            pair_out[s] = kept[s, 1 - core].astype(BF16)
            send(pair_out.at[s], pair_in.at[s], pair_send.at[s], pair_recv.at[s], sibling)

    def pass_on(chunk):
        for s in range(*CHUNKS[chunk]):
            arrived(pair_in.at[s], pair_recv.at[s])
            both = kept[s, core] + pair_in[s].astype(F32)
            if s == 0:
                return both
            m = MIRROR[s]
            sum_out[s] = both.astype(BF16)
            send(sum_out.at[s], sum_in.at[m], sum_send.at[s], sum_recv.at[m], feat_dev(OFFS[s], q))

    x_wait(0)
    half(0, 0)
    x_local(1, 2, 3, 4)
    half(0, 1)
    scores(0)
    x_wait(1, 2)
    half(1, 0)
    total = pass_on(0)
    x_local(5, 6, 7)
    half(1, 1)
    scores(1)
    x_wait(3, 4)
    half(2, 0)
    pass_on(1)
    half(2, 1)
    scores(2)
    x_wait(5, 6)
    half(3, 0)
    pass_on(2)
    pl.semaphore_wait(far_z, 2)
    half(3, 1)
    scores(3)
    x_wait(7)
    half(4, 0)
    pass_on(3)
    half(4, 1)
    scores(4)

    local[4].wait()
    local[5].wait()
    ro = readout[...]
    ro_hi = ro.astype(BF16)
    rest = ro - ro_hi.astype(F32)
    ro_mid = rest.astype(BF16)
    ro_lo = (rest - ro_mid.astype(F32)).astype(BF16)
    x0 = x_all[0].reshape(128, x_all.shape[-1])
    linear = (
        lax.dot_general(ro_hi, x0, nt, preferred_element_type=F32)
        + lax.dot_general(ro_mid, x0, nt, preferred_element_type=F32)
        + lax.dot_general(ro_lo, x0, nt, preferred_element_type=F32)
    )
    linear = jnp.concatenate([linear, jnp.zeros((ROWS - classes, 128), F32)], axis=0)
    pass_on(4)

    for s in range(1, 8):
        arrived(sum_in.at[s], sum_recv.at[s])
        total = total + sum_in[s].astype(F32)
    loc[0] = total.astype(BF16)
    send(loc.at[0], loc.at[2], loc_send.at[0], loc_recv.at[2], neighbour)
    send(loc.at[0], loc.at[3], loc_send.at[1], loc_recv.at[3], across)
    send(loc.at[0], loc.at[1], loc_send.at[2], loc_recv.at[1], sibling)
    for k in range(1, 4):
        arrived(loc.at[k], loc_recv.at[k])
    final[core] = loc[0].astype(F32) + loc[2].astype(F32)
    final[1 - core] = loc[1].astype(F32) + loc[3].astype(F32)
    total = final[...].reshape(ROWS, 128)
    rows = lax.broadcasted_iota(jnp.int32, (ROWS, 128), 0)
    inside = rows < classes
    value = jnp.where(inside, total * (1.0 / math.sqrt(feat_total)) + linear, -1e30)
    value = jnp.exp(value - jnp.max(value, axis=0, keepdims=True))
    probs = value / jnp.sum(value, axis=0, keepdims=True)
    label = labels[pl.ds(z, 1), :]
    residual = jnp.where(rows == label, probs - 1.0, probs)
    res_all[0] = residual.astype(BF16).reshape(2, ROWS // 2, 128)

    for s in range(1, 8):
        m = MIRROR[s]
        send(res_all.at[0, core], res_all.at[m, core], res_send.at[s], res_recv.at[m], feat_dev(OFFS[s], q))
    for s in range(1, 8):
        piece = res_all.at[s, core]
        arrived(piece, res_recv.at[s])
        send(piece, piece, res_pass.at[s], res_got.at[s], sibling)
    for s in range(8):
        if s:
            arrived(res_all.at[s, 1 - core], res_got.at[s])
        res_t[:, s * 128 : (s + 1) * 128] = res_all[s].reshape(ROWS, 128)

    cols_each = out_ref.shape[1]

    def grad_block(k):
        cols = pl.ds(pl.multiple_of(frame_dev(k) * cols_each, cols_each), cols_each)
        return jnp.dot(res_t[...], feats[:, cols], preferred_element_type=F32)

    back = [0] + [(k // 4) * 4 + (4 - k % 4) % 4 for k in range(1, 8)]
    opposite = {"frames": frame_dev(4)}

    def grad_send_blocks(dy):
        far, near = grad_block(4 + dy), grad_block(dy)
        gx_out[dy] = far[:, :XF].astype(BF16)
        send(gx_out.at[dy], gx_in.at[dy], gx_send.at[dy], gx_recv.at[dy], opposite)
        kx[dy] = near[:, :XF]
        if dy:
            gy_out[dy, 0] = near[:, XF:].astype(BF16)
            gy_out[dy, 1] = far[:, XF:].astype(BF16)
            send(gy_out.at[dy], gy_in.at[4 - dy], gy_send.at[dy], gy_recv.at[4 - dy], {"frames": frame_dev(dy)})
        else:
            ky[0] = near[:, XF:]
            ky[1] = far[:, XF:]

    grad_send_blocks(2)

    pl.semaphore_wait(far_x, 1)
    ro_pad[...] = jnp.zeros_like(ro_pad)
    depth = x_all.shape[-1]
    ro_pad[0:ROWS, 0:depth] = jnp.dot(res_t[...], x_all[...].reshape(1024, depth), preferred_element_type=F32)
    ro_mine = ro_pad[pl.ds(pl.multiple_of(z * 32, 32), 32), pl.ds(pl.multiple_of(core * 256, 256), 256)]
    ro_out[...] = ro_mine.astype(BF16)
    for k in range(1, 8):
        b = back[k]
        send(ro_out, ro_in.at[b], ro_send.at[k], ro_recv.at[b], {"frames": frame_dev(k)})

    for dy in (1, 3, 0):
        grad_send_blocks(dy)

    def along_y(dy):
        arrived(gx_in.at[dy], gx_recv.at[dy])
        cy_out[dy] = (kx[dy] + gx_in[dy].astype(F32)).astype(BF16)
        send(cy_out.at[dy], cy_in.at[4 - dy], cy_send.at[dy], cy_recv.at[4 - dy], {"frames": frame_dev(dy)})

    along_y(2)
    rest_own, rest_far = ky[0], ky[1]
    for dy in (1, 3, 2):
        arrived(gy_in.at[dy], gy_recv.at[dy])
        rest_own = rest_own + gy_in[dy, 0].astype(F32)
        rest_far = rest_far + gy_in[dy, 1].astype(F32)
    cx[0] = rest_far.astype(BF16)
    send(cx.at[0], cx.at[1], cx_send.at[0], cx_recv.at[0], opposite)
    along_y(1)
    for k in range(1, 8):
        arrived(ro_in.at[k], ro_recv.at[k])
        ro_mine = ro_mine + ro_in[k].astype(F32)
    ro_all[z, core] = ro_mine.astype(BF16)
    mine = ro_all.at[z, core]
    for s in range(1, 8):
        send(mine, mine, all_send.at[s], all_recv.at[MIRROR[s]], feat_dev(OFFS[s], q))
    send(mine, mine, all_pass.at[0], all_got.at[0], sibling)
    along_y(3)

    arrived(gx_in.at[0], gx_recv.at[0])
    own_grad = kx[0] + gx_in[0].astype(F32)
    arrived(cx.at[1], cx_recv.at[0])
    rest_own = rest_own + cx[1].astype(F32)
    for dy in (2, 1, 3):
        arrived(cy_in.at[dy], cy_recv.at[dy])
        own_grad = own_grad + cy_in[dy].astype(F32)
    own_grad = jnp.concatenate([own_grad, rest_own], axis=1)
    cols = pl.ds(pl.multiple_of(group * cols_each, cols_each), cols_each)
    stepped = w[:, cols] - (5.0 / math.sqrt(batch)) * own_grad[:classes]
    trimmed = stepped - jnp.clip(stepped, -1.0, 1.0)
    part = jnp.sum(trimmed * trimmed, axis=0, keepdims=True)
    part = part[:, 0:128] + part[:, 128:256] + part[:, 256:384] + part[:, 384:512]
    norm_out[...] = jnp.broadcast_to(part, (8, 128))
    for k in range(1, 8):
        b = back[k]
        send(norm_out, norm_in.at[b], norm_send.at[k], norm_recv.at[b], {"frames": frame_dev(k)})
    for s in range(1, 8):
        piece = ro_all.at[(z + OFFS[s] + 8) % 8, core]
        arrived(piece, all_recv.at[s])
        send(piece, piece, all_pass.at[s], all_got.at[s], sibling)
    for s in range(8):
        arrived(ro_all.at[(z + OFFS[s] + 8) % 8, 1 - core], all_got.at[s])
    for i in range(0, classes, 32):
        n = min(32, classes - i)
        grad = jnp.concatenate([ro_all[i // 32, k] for k in range(2)], axis=1).astype(F32)
        readout_out_ref[i : i + n, :] = ro[i : i + n] - (3.0 / math.sqrt(batch)) * grad[:n, :depth]
    for k in range(1, 8):
        arrived(norm_in.at[k], norm_recv.at[k])
        part = part + norm_in[k, 0:1, :]
    norm = jnp.sqrt(jnp.sum(part, axis=1, keepdims=True) + 1e-6)
    limit = 1.5 * math.sqrt(w.shape[0] * w.shape[1])
    out_ref[...] = trimmed * jnp.maximum(0.0, 1.0 - limit / norm)

    for copy in sends:
        copy.wait_send()


def body(frames_in, labels, projection, kernel_scale, shift, weights, readout):
    n_feat, n_frames = lax.axis_size("feat"), lax.axis_size("frames")
    rows, depth = frames_in.shape
    classes, columns = weights.shape
    batch = labels.shape[0] * n_frames
    each = columns // n_frames
    vmem = pl.BlockSpec(memory_space=pltpu.VMEM)
    hbm = pl.BlockSpec(memory_space=pl.ANY)
    dma = pltpu.SemaphoreType.DMA
    return pl.pallas_call(
        functools.partial(kernel, batch, columns * n_feat, classes),
        out_shape=(
            pltpu.VMEM((classes, each), F32),
            pltpu.VMEM(readout.shape, F32),
        ),
        in_specs=[pl.BlockSpec(memory_space=pltpu.SMEM)] + [hbm] * 6,
        out_specs=(vmem, vmem),
        scratch_shapes=[
            pltpu.VMEM((depth, columns), BF16),
            pltpu.VMEM((classes, columns), F32),
            pltpu.VMEM((8, 128), jnp.int32),
            pltpu.VMEM((1, columns), F32),
            pltpu.VMEM(readout.shape, F32),
            pltpu.VMEM((ROWS, columns), BF16),
            pltpu.VMEM((8, 4, rows, depth), BF16),
            pltpu.VMEM((1024, columns), BF16),
            pltpu.VMEM((8, 2, ROWS // 2, 128), F32),
            pltpu.VMEM((8, ROWS // 2, 128), BF16),
            pltpu.VMEM((8, ROWS // 2, 128), BF16),
            pltpu.VMEM((8, ROWS // 2, 128), BF16),
            pltpu.VMEM((8, ROWS // 2, 128), BF16),
            pltpu.VMEM((4, ROWS // 2, 128), BF16),
            pltpu.VMEM((2, ROWS // 2, 128), F32),
            pltpu.VMEM((8, 2, ROWS // 2, 128), BF16),
            pltpu.VMEM((ROWS, 1024), BF16),
            pltpu.VMEM((4, ROWS, XF), BF16),
            pltpu.VMEM((4, ROWS, XF), BF16),
            pltpu.VMEM((4, 2, ROWS, each - XF), BF16),
            pltpu.VMEM((4, 2, ROWS, each - XF), BF16),
            pltpu.VMEM((4, ROWS, XF), BF16),
            pltpu.VMEM((4, ROWS, XF), BF16),
            pltpu.VMEM((2, ROWS, each - XF), BF16),
            pltpu.VMEM((4, ROWS, XF), F32),
            pltpu.VMEM((2, ROWS, each - XF), F32),
            pltpu.VMEM((256, 512), F32),
            pltpu.VMEM((32, 256), BF16),
            pltpu.VMEM((8, 32, 256), BF16),
            pltpu.VMEM((8, 2, 32, 256), BF16),
            pltpu.VMEM((8, 128), F32),
            pltpu.VMEM((8, 8, 128), F32),
            dma((6,)),
            pltpu.SemaphoreType.REGULAR,
            pltpu.SemaphoreType.REGULAR,
            dma((32,)), dma((8, 4)),
            dma((8,)), dma((8,)),
            dma((8,)), dma((8,)),
            dma((3,)), dma((4,)),
            dma((8,)), dma((8,)), dma((8,)), dma((8,)),
            dma((4,)), dma((4,)),
            dma((4,)), dma((4,)),
            dma((4,)), dma((4,)),
            dma((1,)), dma((1,)),
            dma((8,)), dma((8,)),
            dma((8,)), dma((8,)), dma((8,)), dma((8,)),
            dma((8,)), dma((8,)),
        ],
        compiler_params=pltpu.CompilerParams(
            collective_id=0, has_side_effects=True, vmem_limit_bytes=56 * 2**20
        ),
        name="fourier_step",
    )(kernel_scale, frames_in, projection, weights, labels.reshape(8, 128), shift.reshape(1, -1), readout)


def solution(mesh):
    return jax.shard_map(
        body,
        mesh=mesh,
        in_specs=(
            P(("frames", "feat"), None),
            P("frames"),
            P(None, "feat"),
            P("feat"),
            P("feat"),
            P(None, "feat"),
            P(),
        ),
        out_specs=(P(None, ("feat", "frames")), P()),
        check_vma=False,
    )
```

```python
import functools
import math

import jax
import jax.numpy as jnp
from jax import lax
from jax.experimental import pallas as pl
from jax.experimental.pallas import tpu as pltpu
from jax.sharding import PartitionSpec as P

MESH = pl.DeviceIdType.MESH
F32, BF16 = jnp.float32, jnp.bfloat16
ROWS = 160
NB = 256
XF = 256

OFFS = (0, 1, -1, 2, -2, 3, -3, 4)
MIRROR = tuple(OFFS.index(-d) if -d in OFFS else OFFS.index(d) for d in OFFS)
CHUNKS = ((0, 1), (1, 3), (3, 5), (5, 7), (7, 8))

COS = (1.4142124652862549, -27.91513442993164, 91.82299041748047, -120.59228515625, 83.1423110961914, -29.799043655395508)


def features_of(product, scale, shift):
    turns = product * scale + shift
    r = turns - jnp.round(turns)
    u = r * r
    acc = COS[-1] * u + COS[-2]
    for c in COS[-3::-1]:
        acc = acc * u + c
    return acc.astype(BF16)


def kernel(
    batch, feat_total, classes,
    scale_ref, x_hbm, proj_hbm, w_hbm, labels_hbm, shift_hbm, readout_hbm,
    out_ref, readout_out_ref,
    proj, w, labels, shift, readout, w_low, x_all, feats, kept, pair_out, pair_in, sum_out, sum_in, loc, final, res_all, res_t,
    gx_out, gx_in, gy_out, gy_in, cy_out, cy_in, cx, kx, ky, ro_pad, ro_out, ro_in, ro_all, norm_out, norm_in,
    local_sem, far_z, far_x, x_send, x_recv, pair_send, pair_recv, sum_send, sum_recv, loc_send, loc_recv, res_send, res_recv, res_pass, res_got,
    gx_send, gx_recv, gy_send, gy_recv, cy_send, cy_recv, cx_send, cx_recv, ro_send, ro_recv, all_send, all_recv, all_pass, all_got, norm_send, norm_recv,
):
    me = lax.axis_index("feat")
    group = lax.axis_index("frames")
    z, q = me // 4, me % 4
    xh, y = group // 4, group % 4
    core = q % 2
    q_sib = q + 1 - 2 * core
    q_x = (q + 2) % 4

    def feat_dev(d, qq):
        return {"feat": ((z + d + 8) % 8) * 4 + qq}

    def frame_dev(k):
        dx, dy = k // 4, k % 4
        return ((xh + dx) % 2) * 4 + (y + dy) % 4

    sibling, neighbour, across = feat_dev(0, q_sib), feat_dev(0, q_x), feat_dev(0, 3 - q)
    sends = []

    def send(src, dst, ssem, rsem, dev):
        copy = pltpu.make_async_remote_copy(
            src_ref=src, dst_ref=dst, send_sem=ssem, recv_sem=rsem, device_id=dev, device_id_type=MESH
        )
        copy.start()
        sends.append(copy)

    def arrived(ref, rsem):
        pltpu.make_async_remote_copy(
            src_ref=ref, dst_ref=ref, send_sem=x_send.at[0], recv_sem=rsem, device_id=sibling, device_id_type=MESH
        ).wait_recv()

    local = [
        pltpu.make_async_copy(src, dst, local_sem.at[i])
        for i, (src, dst) in enumerate(
            ((x_hbm, x_all.at[0, q]), (shift_hbm, shift), (proj_hbm, proj), (w_hbm, w), (labels_hbm, labels), (readout_hbm, readout))
        )
    ]
    for copy in local:
        copy.start()

    barrier = pltpu.get_barrier_semaphore()
    partners = [feat_dev(d, q) for d in OFFS[1:5]] + [neighbour, across, sibling]
    partners += [{"frames": frame_dev(k)} for k in range(1, 5)]
    for dev in partners:
        pl.semaphore_signal(barrier, inc=1, device_id=dev, device_id_type=MESH)
    pl.semaphore_wait(barrier, len(partners))
    for d in (2, -2):
        pl.semaphore_signal(far_z, inc=1, device_id=feat_dev(d, q), device_id_type=MESH)
    pl.semaphore_signal(far_x, inc=1, device_id={"frames": frame_dev(4)}, device_id_type=MESH)

    def half_of(piece, h):
        return piece.at[16 * h : 16 * h + 16]

    def gather_local(s):
        piece = x_all.at[s, q]
        source = piece if s else x_hbm
        if s == 7:
            for h in range(2):
                arrived(half_of(piece, h), x_recv.at[7 - 7 * h, 0])
        elif s:
            arrived(piece, x_recv.at[s, 0])
        if s in (3, 4):
            on = -1 if s == 3 else 1
            send(piece, x_all.at[s + 2, q], x_send.at[s + 2], x_recv.at[s + 2, 0], feat_dev(on, q))
            h = s - 3
            end = half_of(x_all.at[7, q], h)
            send(half_of(piece, h), end, x_send.at[7 * h], x_recv.at[7 - 7 * h, 0], feat_dev(2 * on, q))
        send(source, piece, x_send.at[8 + s], x_recv.at[s, 2], neighbour)
        send(source, piece, x_send.at[24 + s], x_recv.at[s, 3], across)
        send(source, piece, x_send.at[16 + s], x_recv.at[s, 1], sibling)

    def gather_wait(s):
        arrived(x_all.at[s, q_sib], x_recv.at[s, 1])
        arrived(x_all.at[s, q_x], x_recv.at[s, 2])
        arrived(x_all.at[s, 3 - q], x_recv.at[s, 3])

    def x_local(*slots):
        for s in slots:
            gather_local(s)

    def x_wait(*slots):
        for s in slots:
            gather_wait(s)

    gather_local(0)
    for s in (1, 2, 3, 4):
        m = MIRROR[s]
        send(x_hbm, x_all.at[m, q], x_send.at[s], x_recv.at[m, 0], feat_dev(OFFS[s], q))

    w_low[144:ROWS, :] = jnp.zeros((ROWS - 144, w_low.shape[1]), BF16)
    local[3].wait()
    w_low[0:classes, :] = w[...].astype(BF16)
    local[1].wait()
    local[2].wait()
    local[0].wait()

    nt = (((1,), (1,)), ((), ()))
    turn = 1.0 / (2.0 * math.pi)
    scale = scale_ref[0] * turn

    def half(chunk, first):
        lo, hi = CHUNKS[chunk]
        n = (hi - lo) * 128
        xs = x_all[lo:hi].reshape(n, x_all.shape[-1])

        def block(j, carry):
            cols = pl.ds(pl.multiple_of(j * NB, NB), NB)
            product = jnp.dot(xs, proj[:, cols], preferred_element_type=F32)
            feats[lo * 128 : hi * 128, cols] = features_of(product, scale, shift[:, cols] * turn)
            return carry

        count = feats.shape[1] // NB // 2
        lax.fori_loop(first * count, (first + 1) * count, block, 0, unroll=True)

    def scores(chunk):
        lo, hi = CHUNKS[chunk]
        part = lax.dot_general(w_low[...], feats[lo * 128 : hi * 128, :], nt, preferred_element_type=F32)
        for s in range(lo, hi):
            kept[s] = part[:, (s - lo) * 128 : (s - lo + 1) * 128].reshape(2, ROWS // 2, 128)
            pair_out[s] = kept[s, 1 - core].astype(BF16)
            send(pair_out.at[s], pair_in.at[s], pair_send.at[s], pair_recv.at[s], sibling)

    def pass_on(chunk):
        for s in range(*CHUNKS[chunk]):
            arrived(pair_in.at[s], pair_recv.at[s])
            both = kept[s, core] + pair_in[s].astype(F32)
            if s == 0:
                return both
            m = MIRROR[s]
            sum_out[s] = both.astype(BF16)
            send(sum_out.at[s], sum_in.at[m], sum_send.at[s], sum_recv.at[m], feat_dev(OFFS[s], q))

    x_wait(0)
    half(0, 0)
    x_local(1, 2, 3, 4)
    half(0, 1)
    scores(0)
    x_wait(1, 2)
    half(1, 0)
    total = pass_on(0)
    x_local(5, 6, 7)
    half(1, 1)
    scores(1)
    x_wait(3, 4)
    half(2, 0)
    pass_on(1)
    half(2, 1)
    scores(2)
    x_wait(5, 6)
    half(3, 0)
    pass_on(2)
    pl.semaphore_wait(far_z, 2)
    half(3, 1)
    scores(3)
    x_wait(7)
    half(4, 0)
    pass_on(3)
    half(4, 1)
    scores(4)

    local[4].wait()
    local[5].wait()
    ro = readout[...]
    ro_hi = ro.astype(BF16)
    rest = ro - ro_hi.astype(F32)
    ro_mid = rest.astype(BF16)
    ro_lo = (rest - ro_mid.astype(F32)).astype(BF16)
    x0 = x_all[0].reshape(128, x_all.shape[-1])
    linear = (
        lax.dot_general(ro_hi, x0, nt, preferred_element_type=F32)
        + lax.dot_general(ro_mid, x0, nt, preferred_element_type=F32)
        + lax.dot_general(ro_lo, x0, nt, preferred_element_type=F32)
    )
    linear = jnp.concatenate([linear, jnp.zeros((ROWS - classes, 128), F32)], axis=0)
    pass_on(4)

    for s in range(1, 8):
        arrived(sum_in.at[s], sum_recv.at[s])
        total = total + sum_in[s].astype(F32)
    loc[0] = total.astype(BF16)
    send(loc.at[0], loc.at[2], loc_send.at[0], loc_recv.at[2], neighbour)
    send(loc.at[0], loc.at[3], loc_send.at[1], loc_recv.at[3], across)
    send(loc.at[0], loc.at[1], loc_send.at[2], loc_recv.at[1], sibling)
    for k in range(1, 4):
        arrived(loc.at[k], loc_recv.at[k])
    final[core] = loc[0].astype(F32) + loc[2].astype(F32)
    final[1 - core] = loc[1].astype(F32) + loc[3].astype(F32)
    total = final[...].reshape(ROWS, 128)
    rows = lax.broadcasted_iota(jnp.int32, (ROWS, 128), 0)
    inside = rows < classes
    value = jnp.where(inside, total * (1.0 / math.sqrt(feat_total)) + linear, -1e30)
    value = jnp.exp(value - jnp.max(value, axis=0, keepdims=True))
    probs = value / jnp.sum(value, axis=0, keepdims=True)
    label = labels[pl.ds(z, 1), :]
    residual = jnp.where(rows == label, probs - 1.0, probs)
    res_all[0] = residual.astype(BF16).reshape(2, ROWS // 2, 128)

    for s in range(1, 8):
        m = MIRROR[s]
        send(res_all.at[0, core], res_all.at[m, core], res_send.at[s], res_recv.at[m], feat_dev(OFFS[s], q))
    for s in range(1, 8):
        piece = res_all.at[s, core]
        arrived(piece, res_recv.at[s])
        send(piece, piece, res_pass.at[s], res_got.at[s], sibling)
    for s in range(8):
        if s:
            arrived(res_all.at[s, 1 - core], res_got.at[s])
        res_t[:, s * 128 : (s + 1) * 128] = res_all[s].reshape(ROWS, 128)

    cols_each = out_ref.shape[1]

    def grad_block(k):
        cols = pl.ds(pl.multiple_of(frame_dev(k) * cols_each, cols_each), cols_each)
        return jnp.dot(res_t[...], feats[:, cols], preferred_element_type=F32)

    back = [0] + [(k // 4) * 4 + (4 - k % 4) % 4 for k in range(1, 8)]
    opposite = {"frames": frame_dev(4)}

    def grad_send_blocks(dy):
        far, near = grad_block(4 + dy), grad_block(dy)
        gx_out[dy] = far[:, :XF].astype(BF16)
        send(gx_out.at[dy], gx_in.at[dy], gx_send.at[dy], gx_recv.at[dy], opposite)
        kx[dy] = near[:, :XF]
        if dy:
            gy_out[dy, 0] = near[:, XF:].astype(BF16)
            gy_out[dy, 1] = far[:, XF:].astype(BF16)
            send(gy_out.at[dy], gy_in.at[4 - dy], gy_send.at[dy], gy_recv.at[4 - dy], {"frames": frame_dev(dy)})
        else:
            ky[0] = near[:, XF:]
            ky[1] = far[:, XF:]

    grad_send_blocks(2)

    grad_send_blocks(1)
    grad_send_blocks(3)
    pl.semaphore_wait(far_x, 1)
    ro_pad[...] = jnp.zeros_like(ro_pad)
    depth = x_all.shape[-1]
    ro_pad[0:ROWS, 0:depth] = jnp.dot(res_t[...], x_all[...].reshape(1024, depth), preferred_element_type=F32)
    ro_mine = ro_pad[pl.ds(pl.multiple_of(z * 32, 32), 32), pl.ds(pl.multiple_of(core * 256, 256), 256)]
    ro_out[...] = ro_mine.astype(BF16)
    for k in range(1, 8):
        b = back[k]
        send(ro_out, ro_in.at[b], ro_send.at[k], ro_recv.at[b], {"frames": frame_dev(k)})
    grad_send_blocks(0)

    def along_y(dy):
        arrived(gx_in.at[dy], gx_recv.at[dy])
        cy_out[dy] = (kx[dy] + gx_in[dy].astype(F32)).astype(BF16)
        send(cy_out.at[dy], cy_in.at[4 - dy], cy_send.at[dy], cy_recv.at[4 - dy], {"frames": frame_dev(dy)})

    along_y(2)
    rest_own, rest_far = ky[0], ky[1]
    for dy in (1, 3, 2):
        arrived(gy_in.at[dy], gy_recv.at[dy])
        rest_own = rest_own + gy_in[dy, 0].astype(F32)
        rest_far = rest_far + gy_in[dy, 1].astype(F32)
    cx[0] = rest_far.astype(BF16)
    send(cx.at[0], cx.at[1], cx_send.at[0], cx_recv.at[0], opposite)
    along_y(1)
    along_y(3)
    for k in range(1, 8):
        arrived(ro_in.at[k], ro_recv.at[k])
        ro_mine = ro_mine + ro_in[k].astype(F32)
    ro_all[z, core] = ro_mine.astype(BF16)
    mine = ro_all.at[z, core]
    for s in range(1, 8):
        send(mine, mine, all_send.at[s], all_recv.at[MIRROR[s]], feat_dev(OFFS[s], q))
    send(mine, mine, all_pass.at[0], all_got.at[0], sibling)

    arrived(gx_in.at[0], gx_recv.at[0])
    own_grad = kx[0] + gx_in[0].astype(F32)
    arrived(cx.at[1], cx_recv.at[0])
    rest_own = rest_own + cx[1].astype(F32)
    for dy in (2, 1, 3):
        arrived(cy_in.at[dy], cy_recv.at[dy])
        own_grad = own_grad + cy_in[dy].astype(F32)
    own_grad = jnp.concatenate([own_grad, rest_own], axis=1)
    cols = pl.ds(pl.multiple_of(group * cols_each, cols_each), cols_each)
    stepped = w[:, cols] - (5.0 / math.sqrt(batch)) * own_grad[:classes]
    trimmed = stepped - jnp.clip(stepped, -1.0, 1.0)
    part = jnp.sum(trimmed * trimmed, axis=0, keepdims=True)
    part = part[:, 0:128] + part[:, 128:256] + part[:, 256:384] + part[:, 384:512]
    norm_out[...] = jnp.broadcast_to(part, (8, 128))
    for k in range(1, 8):
        b = back[k]
        send(norm_out, norm_in.at[b], norm_send.at[k], norm_recv.at[b], {"frames": frame_dev(k)})
    for s in range(1, 8):
        piece = ro_all.at[(z + OFFS[s] + 8) % 8, core]
        arrived(piece, all_recv.at[s])
        send(piece, piece, all_pass.at[s], all_got.at[s], sibling)
    for s in range(8):
        arrived(ro_all.at[(z + OFFS[s] + 8) % 8, 1 - core], all_got.at[s])
    for i in range(0, classes, 32):
        n = min(32, classes - i)
        grad = jnp.concatenate([ro_all[i // 32, k] for k in range(2)], axis=1).astype(F32)
        readout_out_ref[i : i + n, :] = ro[i : i + n] - (3.0 / math.sqrt(batch)) * grad[:n, :depth]
    for k in range(1, 8):
        arrived(norm_in.at[k], norm_recv.at[k])
        part = part + norm_in[k, 0:1, :]
    norm = jnp.sqrt(jnp.sum(part, axis=1, keepdims=True) + 1e-6)
    limit = 1.5 * math.sqrt(w.shape[0] * w.shape[1])
    out_ref[...] = trimmed * jnp.maximum(0.0, 1.0 - limit / norm)

    for copy in sends:
        copy.wait_send()


def body(frames_in, labels, projection, kernel_scale, shift, weights, readout):
    n_feat, n_frames = lax.axis_size("feat"), lax.axis_size("frames")
    rows, depth = frames_in.shape
    classes, columns = weights.shape
    batch = labels.shape[0] * n_frames
    each = columns // n_frames
    vmem = pl.BlockSpec(memory_space=pltpu.VMEM)
    hbm = pl.BlockSpec(memory_space=pl.ANY)
    dma = pltpu.SemaphoreType.DMA
    return pl.pallas_call(
        functools.partial(kernel, batch, columns * n_feat, classes),
        out_shape=(
            pltpu.VMEM((classes, each), F32),
            pltpu.VMEM(readout.shape, F32),
        ),
        in_specs=[pl.BlockSpec(memory_space=pltpu.SMEM)] + [hbm] * 6,
        out_specs=(vmem, vmem),
        scratch_shapes=[
            pltpu.VMEM((depth, columns), BF16),
            pltpu.VMEM((classes, columns), F32),
            pltpu.VMEM((8, 128), jnp.int32),
            pltpu.VMEM((1, columns), F32),
            pltpu.VMEM(readout.shape, F32),
            pltpu.VMEM((ROWS, columns), BF16),
            pltpu.VMEM((8, 4, rows, depth), BF16),
            pltpu.VMEM((1024, columns), BF16),
            pltpu.VMEM((8, 2, ROWS // 2, 128), F32),
            pltpu.VMEM((8, ROWS // 2, 128), BF16),
            pltpu.VMEM((8, ROWS // 2, 128), BF16),
            pltpu.VMEM((8, ROWS // 2, 128), BF16),
            pltpu.VMEM((8, ROWS // 2, 128), BF16),
            pltpu.VMEM((4, ROWS // 2, 128), BF16),
            pltpu.VMEM((2, ROWS // 2, 128), F32),
            pltpu.VMEM((8, 2, ROWS // 2, 128), BF16),
            pltpu.VMEM((ROWS, 1024), BF16),
            pltpu.VMEM((4, ROWS, XF), BF16),
            pltpu.VMEM((4, ROWS, XF), BF16),
            pltpu.VMEM((4, 2, ROWS, each - XF), BF16),
            pltpu.VMEM((4, 2, ROWS, each - XF), BF16),
            pltpu.VMEM((4, ROWS, XF), BF16),
            pltpu.VMEM((4, ROWS, XF), BF16),
            pltpu.VMEM((2, ROWS, each - XF), BF16),
            pltpu.VMEM((4, ROWS, XF), F32),
            pltpu.VMEM((2, ROWS, each - XF), F32),
            pltpu.VMEM((256, 512), F32),
            pltpu.VMEM((32, 256), BF16),
            pltpu.VMEM((8, 32, 256), BF16),
            pltpu.VMEM((8, 2, 32, 256), BF16),
            pltpu.VMEM((8, 128), F32),
            pltpu.VMEM((8, 8, 128), F32),
            dma((6,)),
            pltpu.SemaphoreType.REGULAR,
            pltpu.SemaphoreType.REGULAR,
            dma((32,)), dma((8, 4)),
            dma((8,)), dma((8,)),
            dma((8,)), dma((8,)),
            dma((3,)), dma((4,)),
            dma((8,)), dma((8,)), dma((8,)), dma((8,)),
            dma((4,)), dma((4,)),
            dma((4,)), dma((4,)),
            dma((4,)), dma((4,)),
            dma((1,)), dma((1,)),
            dma((8,)), dma((8,)),
            dma((8,)), dma((8,)), dma((8,)), dma((8,)),
            dma((8,)), dma((8,)),
        ],
        compiler_params=pltpu.CompilerParams(
            collective_id=0, has_side_effects=True, vmem_limit_bytes=56 * 2**20
        ),
        name="fourier_step",
    )(kernel_scale, frames_in, projection, weights, labels.reshape(8, 128), shift.reshape(1, -1), readout)


def solution(mesh):
    return jax.shard_map(
        body,
        mesh=mesh,
        in_specs=(
            P(("frames", "feat"), None),
            P("frames"),
            P(None, "feat"),
            P("feat"),
            P("feat"),
            P(None, "feat"),
            P(),
        ),
        out_specs=(P(None, ("feat", "frames")), P()),
        check_vma=False,
    )
```
